256 devices in a mesh: dp: 8 (over z), cls: 8 (over y, core), feat: 4 (over x).
Axes of the slice: x: 4, y: 4, z: 8, core: 2. Of those that a mesh axis runs over, the one named last changes fastest.
Arguments:
- utter: bfloat16 [65536, 1024], P(('dp', 'cls'), 'feat'), may hold values from -6 to 6
- intents: bfloat16 [524288, 1024], P(('dp', 'cls'), 'feat'), may hold values from -0.1875 to 0.1875
- req_blocks: int32 [512, 16], replicated, may hold values from -1 to 4095, as said below
- req_count: int32 [512], replicated, may hold values from 4 to 16, as said below
- block_home: int32 [4096], replicated, may hold values from 0 to 4095, as said below
- labels: int32 [65536, 2], P(('dp', 'cls')), may hold values from 0 to 524287, as said below
Outputs:
- grad_utter: bfloat16 [65536, 1024], P(('dp', 'cls'), 'feat')
- grad_intents: bfloat16 [524288, 1024], P(('dp', 'cls'), 'feat')
The draws below stay inside these ranges and needn't reach their ends.
Inputs may be any that keep to these rules, and one draw needn't show every extreme that they name: `req_blocks`: on each device along dp+cls the live entries of its 8 lists are distinct blocks, and at most 2 of them have block_home within one device's range of 64 stored blocks; entries at or past req_count are -1. `req_count`: the 8 counts of one device sum to 64. `block_home`: A permutation of the block ids. `labels`: each label lies in a live block of its utterance block's list.
All inputs are finite; a program needn't handle non-finite values.
Results may differ from the reference program's by a relative error of at most 0.0052.
Values may be sent and summed in bfloat16 or wider, within the bound.
A program may use at most 128 MiB of HBM per device.

```python
import jax
import jax.numpy as jnp
import numpy as np
from jax import lax

D = 1024
BLK = 128
BLK_DEV = 64
UB = 128
UBD = 8
MOST = 16
REQ_DEV = 64
NPOS = 2
OWNERS = 64
NBLK = 4096
INTENTS = 524288
UBLOCKS = 512
UTTS = 65536


PATTERNS = np.array([[16, 12, 8, 8, 6, 6, 4, 4], [16, 16, 8, 6, 6, 4, 4, 4], [16, 10, 10, 8, 6, 6, 4, 4], [16, 8, 8, 8, 8, 8, 4, 4]], dtype=np.int32)


def distinct_order(key, shape):
    length = shape[-1]
    noise = jax.random.randint(key, shape, 0, 1 << 20)
    return jnp.argsort(noise * length + jnp.arange(length), axis=-1).astype(jnp.int32)


def request_plan(key):
    key_home, key_hot, key_rank, key_pick, key_mix, key_pat, key_order = jax.random.split(key, 7)
    storage = jax.random.permutation(key_home, NBLK).astype(jnp.int32)
    block_of = jnp.argsort(storage).astype(jnp.int32)
    hottest = jax.random.randint(key_hot, (), 0, OWNERS)
    owner_ids = jnp.arange(OWNERS)
    noise = jax.random.randint(key_rank, (OWNERS, OWNERS), 0, 1 << 20) * OWNERS + owner_ids[None, :]
    noise = jnp.where(owner_ids[None, :] == hottest, -1, noise)
    by_rank = jnp.argsort(noise, axis=1).astype(jnp.int32)
    capacity = 2 * REQ_DEV // OWNERS
    quarter = OWNERS // 4
    item_ids = jnp.arange(REQ_DEV)
    first = item_ids < quarter * capacity
    later = item_ids - quarter * capacity
    rank_of = jnp.where(first, item_ids // capacity, quarter + later // (capacity // 2))
    which = jnp.where(first, item_ids % capacity, later % (capacity // 2))
    owner_of = by_rank[:, rank_of]
    picks = distinct_order(key_pick, (OWNERS, OWNERS, BLK_DEV))
    local_of = picks[jnp.arange(OWNERS)[:, None], owner_of, which[None, :]]
    blocks = block_of[owner_of * BLK_DEV + local_of]
    blocks = jnp.take_along_axis(blocks, distinct_order(key_mix, (OWNERS, REQ_DEV)), axis=1)
    choice_ids = jax.random.randint(key_pat, (OWNERS,), 0, PATTERNS.shape[0])
    lengths = jnp.asarray(PATTERNS)[choice_ids]
    lengths = jnp.take_along_axis(lengths, distinct_order(key_order, (OWNERS, UBD)), axis=1)
    starts = jnp.cumsum(lengths, axis=1) - lengths
    column = jnp.arange(MOST)
    position = jnp.minimum(starts[:, :, None] + column[None, None, :], REQ_DEV - 1)
    chosen = jnp.take_along_axis(blocks, position.reshape(OWNERS, UBD * MOST), axis=1).reshape(OWNERS, UBD, MOST)
    chosen = jnp.where(column[None, None, :] < lengths[:, :, None], chosen, -1)
    return (storage, chosen.reshape(UBLOCKS, MOST).astype(jnp.int32), lengths.reshape(UBLOCKS).astype(jnp.int32))


def draw_req_blocks(key, part):
    storage, chosen, lengths = request_plan(key)
    return chosen


def draw_req_count(key, part):
    storage, chosen, lengths = request_plan(key)
    return lengths


def draw_block_home(key, part):
    storage, chosen, lengths = request_plan(key)
    return storage


def draw_labels(key, part):
    storage, chosen, lengths = request_plan(key)
    key = jax.random.fold_in(key, 4)
    key_pos, key_in = jax.random.split(key)
    owner_block = jnp.arange(UTTS) // UB
    position = jax.random.randint(key_pos, (UTTS, NPOS), 0, lengths[owner_block][:, None])
    within = jax.random.randint(key_in, (UTTS, NPOS), 0, BLK)
    return (chosen[owner_block[:, None], position] * BLK + within).astype(jnp.int32)


def levels(key, extent, shards, least, largest):
    def one(dim, parts):
        draws = jax.random.uniform(jax.random.fold_in(jax.random.fold_in(key, 6), dim), (parts,), jnp.float32, least / len(shards), largest / len(shards))
        return jnp.repeat(jnp.exp(draws), extent[dim] // parts).reshape((-1,) + (1,) * (len(extent) - dim - 1))

    factor_of = one(*shards[0])
    for cut in shards[1:]:
        factor_of = factor_of * one(*cut)
    return factor_of


def gaussian(rng, extent, spread, limit, cuts=(), kind=jnp.bfloat16):
    factor_of = levels(rng, extent, cuts, -0.22, 0.18) if cuts else 1.0
    result = jax.random.normal(rng, extent, jnp.float32) * spread * factor_of
    return jnp.minimum(jnp.maximum(result, -limit), limit).astype(kind)


def setup_inputs(seed: int = 0) -> dict:
    arg_keys = jax.random.split(jax.random.key(seed), 7)
    return {
        "utter": gaussian(arg_keys[0], (UTTS, D), 1.0, 6.0, ((0, 64), (1, 4))),
        "intents": gaussian(arg_keys[1], (INTENTS, D), D ** -0.5, 0.1875, ((0, 64), (1, 4))),
        "req_blocks": draw_req_blocks(jax.random.fold_in(arg_keys[6], 71), 0),
        "req_count": draw_req_count(jax.random.fold_in(arg_keys[6], 71), 0),
        "block_home": draw_block_home(jax.random.fold_in(arg_keys[6], 71), 0),
        "labels": draw_labels(jax.random.fold_in(arg_keys[6], 71), 0),
    }


GAMMA = 4.0
MARGIN = 0.25


def margin_slope(scores, blocks, live_count, label_ids):
    list_len = blocks.shape[1]
    block_width = scores.shape[2] // list_len
    within = jnp.arange(block_width)
    matched = (blocks[:, None, :, None, None] == (label_ids // block_width)[:, :, None, None, :]) & (within[None, None, None, :, None] == (label_ids % block_width)[:, :, None, None, :])
    target = jnp.any(matched, axis=4).reshape(scores.shape).astype(jnp.float32)
    live_blocks = jnp.arange(list_len)[None, :] < live_count[:, None]
    alive_cols = jnp.repeat(live_blocks, block_width, axis=1).astype(jnp.float32)
    logits = GAMMA * scores
    derivative = (1.0 - target) * jax.nn.sigmoid(logits + MARGIN) - target * jax.nn.sigmoid(MARGIN - logits)
    return (GAMMA * alive_cols[:, None, :] * derivative / live_count.astype(jnp.float32)[:, None, None]).astype(jnp.bfloat16)


def reference(utter, intents, req_blocks, req_count, block_home, labels):
    stored = intents.reshape(NBLK, BLK, D)
    stored_at = block_home[jnp.maximum(req_blocks, 0)]
    live_all = jnp.arange(MOST)[None, :] < req_count[:, None]

    def step(summed, pieces):
        utt_rows, blocks, places, live_blocks, live_count, label_ids = pieces
        w_rows = stored[places].reshape(MOST * BLK, D)
        scores = jnp.dot(utt_rows, w_rows.T, preferred_element_type=jnp.float32)
        grad_scores = margin_slope(scores[None], blocks[None], live_count[None], label_ids[None])[0]
        grad_rows = jnp.dot(grad_scores, w_rows, preferred_element_type=jnp.float32).astype(jnp.bfloat16)
        contribution = jnp.dot(grad_scores.T, utt_rows, preferred_element_type=jnp.float32).astype(jnp.bfloat16)
        contribution = lax.optimization_barrier(contribution)
        target_rows = jnp.where(live_blocks, places, NBLK)
        summed = summed.at[target_rows].add(contribution.reshape(MOST, BLK, D).astype(jnp.float32), mode="drop")
        return summed, grad_rows

    pieces = (utter.reshape(UBLOCKS, UB, D), req_blocks, stored_at, live_all, req_count, labels.reshape(UBLOCKS, UB, NPOS))
    summed, grad_rows = lax.scan(step, jnp.zeros((NBLK, BLK, D), jnp.float32), pieces)
    return grad_rows.reshape(UTTS, D), summed.reshape(INTENTS, D).astype(jnp.bfloat16)
```

```python
import functools

import jax
import jax.numpy as jnp
import numpy as np
from jax import lax
from jax.experimental import pallas as pl
from jax.experimental.pallas import tpu as pltpu
from jax.sharding import PartitionSpec as P

BLK = 128
BLK_DEV = 64
UB = 128
UBD = 8
MOST = 16
GAMMA = 4.0
MARGIN = 0.25

NY, NZ = 4, 8
CHIPS = NY * NZ
SLOTS = 4
DEPTH = 4
LAG = 3
HALVES = 2
PART = UBD // HALVES
MESH = pl.DeviceIdType.MESH

CYCLES = (
    (0, 8, 9, 1, 25, 24, 16, 17, 18, 10, 2, 26, 27, 19, 11, 3, 4, 12, 20, 28, 29, 5, 13, 21, 22, 30, 6, 14, 15, 23, 31, 7),
    (0, 1, 2, 3, 27, 28, 4, 5, 6, 7, 15, 8, 16, 23, 22, 14, 13, 12, 11, 10, 9, 17, 25, 26, 18, 19, 20, 21, 29, 30, 31, 24),
)


def _tables():
    link = np.zeros((2, CHIPS), np.int64)
    order = np.zeros((CHIPS, 2, CHIPS), np.int32)
    for c, cycle in enumerate(CYCLES):
        for i, chip in enumerate(cycle):
            after, before = cycle[(i + 1) % CHIPS], cycle[(i - 1) % CHIPS]
            link[c, chip] = (after * CHIPS + before) * 2 + i % 2
            for n in range(CHIPS):
                source = cycle[(i - n) % CHIPS] if (i + n) % 2 == 0 else cycle[(i + n) % CHIPS]
                order[chip, c, n] = (source % NZ) * (2 * NY) + (source // NZ) * 2 + c
    return link, order


LINK, ORDER = _tables()


def ring_kernel(
    ku_ref, lb_ref, bid_ref, scale_ref, utter_ref, lab_ref, intents_ref,
    gu_ref, con_ref,
    ag, aglab, rs, w, ucur, usel, labsel, part, recv, gs, gbuf, cst,
    sem_in, sem_w, ag_send, ag_recv, lab_send, lab_recv, rs_send, rs_recv,
    part_send, part_recv, gs_send, gs_recv, con_send, con_recv, con_loc, sem_out,
):
    z = lax.axis_index("dp")
    cl = lax.axis_index("cls")
    x = lax.axis_index("feat")
    y = cl // 2
    core = cl % 2
    chip = y * NZ + z
    code = chip + core * CHIPS
    packed = jnp.int32(0)
    for c in range(2):
        for k in range(CHIPS):
            packed = packed + jnp.where(code == c * CHIPS + k, jnp.int32(int(LINK[c, k])), jnp.int32(0))
    after = packed // (2 * CHIPS)
    before = (packed // 2) % CHIPS
    parity = packed % 2

    def device_of(c):
        return (c % NZ, (c // NZ) * 2 + core, x)

    def down(n):
        odd = (parity + n) % 2
        return device_of(after + odd * (before - after))

    other = (z, y * 2 + (1 - core), x)

    def peer(o):
        return (z, cl, (x + o) % 4)

    def ag_copy(n, h):
        return pltpu.make_async_remote_copy(
            src_ref=ag.at[n, pl.ds(h * PART, PART)], dst_ref=ag.at[n + 1, pl.ds(h * PART, PART)],
            send_sem=ag_send.at[n, h], recv_sem=ag_recv.at[n + 1, h], device_id=down(n), device_id_type=MESH)

    def ag_wait(n, h):
        pltpu.make_async_remote_copy(
            src_ref=ag.at[n, pl.ds(h * PART, PART)], dst_ref=ag.at[n, pl.ds(h * PART, PART)],
            send_sem=ag_send.at[n, h], recv_sem=ag_recv.at[n, h], device_id=down(n), device_id_type=MESH).wait_recv()

    def lab_copy(n):
        return pltpu.make_async_remote_copy(
            src_ref=aglab.at[n], dst_ref=aglab.at[n + 1],
            send_sem=lab_send.at[n], recv_sem=lab_recv.at[n + 1], device_id=down(n), device_id_type=MESH)

    def lab_wait(n):
        pltpu.make_async_remote_copy(
            src_ref=aglab.at[n], dst_ref=aglab.at[n],
            send_sem=lab_send.at[n], recv_sem=lab_recv.at[n], device_id=down(n), device_id_type=MESH).wait_recv()

    def rs_copy(m, h):
        return pltpu.make_async_remote_copy(
            src_ref=rs.at[m - 1, pl.ds(h * PART, PART)], dst_ref=rs.at[m, pl.ds(h * PART, PART)],
            send_sem=rs_send.at[m - 1, h], recv_sem=rs_recv.at[m, h], device_id=down(m), device_id_type=MESH)

    def rs_wait(m, h):
        pltpu.make_async_remote_copy(
            src_ref=rs.at[m - 1, pl.ds(h * PART, PART)], dst_ref=rs.at[m - 1, pl.ds(h * PART, PART)],
            send_sem=rs_send.at[m - 1, h], recv_sem=rs_recv.at[m - 1, h], device_id=down(m), device_id_type=MESH).wait_recv()

    def part_copy(n, o):
        to = (x + o) % 4
        return pltpu.make_async_remote_copy(
            src_ref=part.at[n % DEPTH, to], dst_ref=recv.at[n % DEPTH, o - 1],
            send_sem=part_send.at[n % DEPTH, o - 1], recv_sem=part_recv.at[n % DEPTH, o - 1],
            device_id=peer(o), device_id_type=MESH)

    def gs_copy(m, o):
        return pltpu.make_async_remote_copy(
            src_ref=gs.at[m % DEPTH, x], dst_ref=gs.at[m % DEPTH, x],
            send_sem=gs_send.at[m % DEPTH, o - 1], recv_sem=gs_recv.at[m % DEPTH, o - 1],
            device_id=peer(o), device_id_type=MESH)

    def gs_wait(m, o):
        source = (x + 4 - o) % 4
        pltpu.make_async_remote_copy(
            src_ref=gs.at[m % DEPTH, source], dst_ref=gs.at[m % DEPTH, source],
            send_sem=gs_send.at[m % DEPTH, o - 1], recv_sem=gs_recv.at[m % DEPTH, o - 1],
            device_id=peer(o), device_id_type=MESH).wait_recv()

    def con_far(m):
        return pltpu.make_async_remote_copy(
            src_ref=cst.at[m % DEPTH, pl.ds(2 * (1 - core), 2)], dst_ref=con_ref.at[core, m],
            send_sem=con_send.at[m % DEPTH], recv_sem=con_recv.at[m], device_id=other, device_id_type=MESH)

    def con_far_wait(m):
        pltpu.make_async_remote_copy(
            src_ref=cst.at[m % DEPTH, pl.ds(2 * (1 - core), 2)], dst_ref=con_ref.at[1 - core, m],
            send_sem=con_send.at[m % DEPTH], recv_sem=con_recv.at[m], device_id=other, device_id_type=MESH).wait_recv()

    def con_near(m):
        return pltpu.make_async_copy(
            cst.at[m % DEPTH, pl.ds(2 * core, 2)], con_ref.at[core, m], con_loc.at[m % DEPTH])

    own_u = pltpu.make_async_copy(utter_ref, ag.at[0], sem_in.at[0])
    own_l = pltpu.make_async_copy(lab_ref, aglab.at[0], sem_in.at[1])
    own_w = pltpu.make_async_copy(intents_ref, w.at[pl.ds(core * BLK_DEV, BLK_DEV)], sem_in.at[2])
    far_w = pltpu.make_async_remote_copy(
        src_ref=intents_ref, dst_ref=w.at[pl.ds(core * BLK_DEV, BLK_DEV)],
        send_sem=sem_w.at[0], recv_sem=sem_w.at[1], device_id=other, device_id_type=MESH)
    far_w_in = pltpu.make_async_remote_copy(
        src_ref=intents_ref, dst_ref=w.at[pl.ds((1 - core) * BLK_DEV, BLK_DEV)],
        send_sem=sem_w.at[0], recv_sem=sem_w.at[1], device_id=other, device_id_type=MESH)
    own_u.start()
    own_l.start()
    own_w.start()
    rs[0] = jnp.zeros(rs.shape[1:], rs.dtype)

    barrier = pltpu.get_barrier_semaphore()
    for device in (device_of(after), device_of(before), other, peer(1), peer(2), peer(3)):
        pl.semaphore_signal(barrier, inc=1, device_id=device, device_id_type=MESH)
    pl.semaphore_wait(barrier, 6)
    far_w.start()
    own_u.wait()
    own_l.wait()

    def stage_ag(n, h):
        @pl.when((n >= 1) & (n < CHIPS))
        def _():
            ag_wait(n, h)
            if h == 0:
                lab_wait(n)

        @pl.when(n < CHIPS - 1)
        def _():
            ag_copy(n, h).start()
            if h == 0:
                lab_copy(n).start()

    def stage_rs(m, h):
        @pl.when((m >= 1) & (m <= CHIPS))
        def _():
            @pl.when(m >= 2)
            def _():
                rs_wait(m, h)

            row = m % CHIPS
            slot = jnp.where(row == 0, 2, m % 2)
            kus = [ku_ref[row * SLOTS + s] for s in range(SLOTS)]
            for j in range(h * PART, (h + 1) * PART):
                total = rs[m - 1, j].astype(jnp.float32)
                for s in range(SLOTS):
                    total = total + gbuf[slot, s] * (kus[s] == j).astype(jnp.float32)
                rs[m - 1, j] = total.astype(jnp.bfloat16)

            @pl.when(m < CHIPS)
            def _():
                rs_copy(m, h).start()

    def stage_scores(n):
        @pl.when(n < CHIPS)
        def _():
            d = n % DEPTH

            @pl.when(n >= DEPTH)
            def _():
                for o in range(1, 4):
                    part_copy(n, o).wait_send()

            for j in range(UBD):
                ucur[j] = ag[n, j]
            mine = ku_ref[n * SLOTS + x]
            rows = lax.broadcasted_iota(jnp.int32, (UBD, UB), 0)
            for k in range(2):
                labs = aglab[n, k * UBD:(k + 1) * UBD]
                labsel[d, k:k + 1] = jnp.sum(jnp.where(rows == mine, labs, 0), axis=0, keepdims=True)
            for s in range(SLOTS):
                block = ucur[ku_ref[n * SLOTS + s]]
                usel[d, s] = block
                part[d, s] = lax.dot_general(
                    w[lb_ref[n * SLOTS + s]], block, (((1,), (1,)), ((), ())),
                    preferred_element_type=jnp.float32)
            for o in range(1, 4):
                part_copy(n, o).start()

    def stage_slope(m):
        @pl.when((m >= 0) & (m < CHIPS))
        def _():
            d = m % DEPTH

            @pl.when(m >= DEPTH)
            def _():
                for o in range(1, 4):
                    gs_copy(m, o).wait_send()

            total = part[d, x]
            for o in range(1, 4):
                part_copy(m, o).wait_recv()
                total = total + recv[d, o - 1]
            logits = GAMMA * total
            ids = lax.broadcasted_iota(jnp.int32, (BLK, UB), 0) + bid_ref[m * SLOTS + x] * BLK
            hit = (ids == labsel[d, 0:1]) | (ids == labsel[d, 1:2])
            slope = jax.nn.sigmoid(jnp.where(hit, MARGIN - logits, logits + MARGIN))
            slope = jnp.where(hit, -slope, slope) * scale_ref[m * SLOTS + x]
            gs[d, x] = slope.astype(jnp.bfloat16)
            for o in range(1, 4):
                gs_copy(m, o).start()

    def stage_grads(m):
        @pl.when((m >= 0) & (m < CHIPS))
        def _():
            d = m % DEPTH
            slot = jnp.where(m == 0, 2, m % 2)

            @pl.when(m >= DEPTH)
            def _():
                con_far(m).wait_send()
                con_near(m).wait()

            for o in range(1, 4):
                gs_wait(m, o)
            for s in range(SLOTS):
                slope = gs[d, s]
                cst[d, s] = jnp.dot(slope, usel[d, s], preferred_element_type=jnp.float32).astype(jnp.bfloat16)
                gbuf[slot, s] = lax.dot_general(
                    slope, w[lb_ref[m * SLOTS + s]], (((0,), (0,)), ((), ())),
                    preferred_element_type=jnp.float32)
            con_far(m).start()
            con_near(m).start()

    def step(n, carry):
        for h in range(HALVES):
            stage_ag(n, h)

            @pl.when(n == 0)
            def _():
                if h == 0:
                    own_w.wait()
                    far_w_in.wait_recv()

            stage_rs(n - LAG, h)
        stage_scores(n)
        stage_slope(n - 1)
        stage_grads(n - 2)
        return carry

    lax.fori_loop(0, CHIPS + LAG + 1, step, 0)

    out = pltpu.make_async_copy(rs.at[CHIPS - 1], gu_ref, sem_out)
    out.start()

    def drain(n, carry):
        for h in range(HALVES):
            ag_copy(n, h).wait_send()
            rs_copy(n + 1, h).wait_send()
        lab_copy(n).wait_send()
        con_far_wait(n)
        return carry

    lax.fori_loop(0, CHIPS - 1, drain, 0)
    con_far_wait(CHIPS - 1)
    for n in range(CHIPS - DEPTH, CHIPS):
        for o in range(1, 4):
            part_copy(n, o).wait_send()
            gs_copy(n, o).wait_send()
        con_far(n).wait_send()
        con_near(n).wait()
    far_w.wait_send()
    out.wait()


def ring(ku, lb, bid, scale, utter, labs, intents):
    width = intents.shape[2]
    block = (UB, width)
    dma = pltpu.SemaphoreType.DMA
    anyspace = pl.BlockSpec(memory_space=pl.ANY)
    smem = pl.BlockSpec(memory_space=pltpu.SMEM)
    return pl.pallas_call(
        ring_kernel,
        out_shape=(
            jax.ShapeDtypeStruct((UBD,) + block, jnp.bfloat16),
            jax.ShapeDtypeStruct((2, CHIPS, 2) + block, jnp.bfloat16),
        ),
        in_specs=[smem] * 4 + [anyspace] * 3,
        out_specs=(anyspace, anyspace),
        scratch_shapes=[
            pltpu.VMEM((CHIPS, UBD) + block, jnp.bfloat16),
            pltpu.VMEM((CHIPS, 2 * UBD, UB), jnp.int32),
            pltpu.VMEM((CHIPS, UBD) + block, jnp.bfloat16),
            pltpu.VMEM((2 * BLK_DEV,) + block, jnp.bfloat16),
            pltpu.VMEM((UBD,) + block, jnp.bfloat16),
            pltpu.VMEM((DEPTH, SLOTS) + block, jnp.bfloat16),
            pltpu.VMEM((DEPTH, 8, UB), jnp.int32),
            pltpu.VMEM((DEPTH, SLOTS, BLK, UB), jnp.float32),
            pltpu.VMEM((DEPTH, 3, BLK, UB), jnp.float32),
            pltpu.VMEM((DEPTH, SLOTS, BLK, UB), jnp.bfloat16),
            pltpu.VMEM((3, SLOTS) + block, jnp.float32),
            pltpu.VMEM((DEPTH, SLOTS) + block, jnp.bfloat16),
            dma((3,)), dma((2,)),
            dma((CHIPS, HALVES)), dma((CHIPS, HALVES)), dma((CHIPS,)), dma((CHIPS,)),
            dma((CHIPS, HALVES)), dma((CHIPS, HALVES)),
            dma((DEPTH, 3)), dma((DEPTH, 3)), dma((DEPTH, 3)), dma((DEPTH, 3)),
            dma((DEPTH,)), dma((CHIPS,)), dma((DEPTH,)), dma,
        ],
        compiler_params=pltpu.CompilerParams(
            collective_id=0, has_side_effects=True, vmem_limit_bytes=60 * 1024 * 1024),
        name="ring",
    )(ku, lb, bid, scale, utter, labs, intents)


CHUNK = 16


def gather_kernel(lb_ref, con_ref, out_ref, acc):
    i = pl.program_id(0)

    @pl.when(i == 0)
    def _():
        acc[...] = jnp.zeros_like(acc)

    for k in range(CHUNK):
        b = lb_ref[i * CHUNK + k]
        acc[b] = acc[b] + con_ref[k].astype(jnp.float32)

    @pl.when(i == pl.num_programs(0) - 1)
    def _():
        out_ref[...] = acc[...].astype(out_ref.dtype)


def gather(lb, con):
    count, width = con.shape[0], con.shape[2]
    return pl.pallas_call(
        gather_kernel,
        grid_spec=pltpu.PrefetchScalarGridSpec(
            num_scalar_prefetch=1,
            grid=(count // CHUNK,),
            in_specs=[pl.BlockSpec((CHUNK, BLK, width), lambda i, t: (i, 0, 0))],
            out_specs=pl.BlockSpec((BLK_DEV, BLK, width), lambda i, t: (0, 0, 0)),
            scratch_shapes=[pltpu.VMEM((BLK_DEV, BLK, width), jnp.float32)],
        ),
        out_shape=jax.ShapeDtypeStruct((BLK_DEV, BLK, width), jnp.bfloat16),
        compiler_params=pltpu.CompilerParams(vmem_limit_bytes=40 * 1024 * 1024),
        name="sum_blocks",
    )(lb, con)


def plan(req_blocks, req_count, block_home):
    z = lax.axis_index("dp")
    cl = lax.axis_index("cls")
    chip = (cl // 2) * NZ + z
    base = (z * 2 * NY + (cl // 2) * 2) * BLK_DEV
    order = lax.dynamic_index_in_dim(jnp.asarray(ORDER), chip, 0, keepdims=False).reshape(2 * CHIPS)
    entries = UBD * MOST
    req = req_blocks.reshape(2 * CHIPS, entries)[order]
    count = req_count.reshape(2 * CHIPS, UBD)[order]
    place = jnp.arange(2 * BLK_DEV)
    ids = jnp.sum(
        jnp.where(block_home[None, :] == base + place[:, None], jnp.arange(block_home.shape[0])[None, :], 0), axis=1)
    local = jnp.sum(jnp.where(req[:, :, None] == ids[None, None, :], place[None, None, :] + 1, 0), axis=2) - 1
    at = jnp.arange(entries)[None, None, :]
    owner = jnp.arange(2)[None, :, None]
    mine = (local[:, None, :] >= 0) & (local[:, None, :] // BLK_DEV == owner)
    first = jnp.min(jnp.where(mine, at, entries), axis=2)
    last = jnp.max(jnp.where(mine, at, -1), axis=2)
    entry = jnp.stack([first, last], axis=2)
    valid = jnp.stack([last >= 0, last > first], axis=2)
    hot = (at[..., None, :] == entry[..., None]) & valid[..., None]
    lb = jnp.sum(jnp.where(hot, local[:, None, None, :], 0), axis=3)
    bid = jnp.sum(jnp.where(hot, req[:, None, None, :], 0), axis=3)
    ku = jnp.where(valid, entry // MOST, 0)
    listed = jnp.sum(jnp.where(ku[..., None] == jnp.arange(UBD), count[:, None, None, :], 0), axis=3)
    scale = jnp.where(valid, GAMMA / listed.astype(jnp.float32), 0.0)
    return ku, lb, bid, scale


def shards(utter, intents, req_blocks, req_count, block_home, labels):
    core = lax.axis_index("cls") % 2
    width = intents.shape[1]
    ku, lb, bid, scale = plan(req_blocks, req_count, block_home)

    def row(t, c):
        return lax.dynamic_index_in_dim(t.reshape(2, CHIPS, SLOTS), c, 0, keepdims=False).reshape(CHIPS * SLOTS)

    labs = labels.reshape(UBD, UB, 2).transpose(2, 0, 1).reshape(2 * UBD, UB)
    grad_utter, con = ring(
        row(ku, core), row(lb, core), row(bid, core), row(scale, core),
        utter.reshape(UBD, UB, width), labs, intents.reshape(BLK_DEV, BLK, width))
    near = lax.dynamic_index_in_dim(lb.reshape(2, CHIPS, 2, 2), core, 2, keepdims=False).reshape(4 * CHIPS) % BLK_DEV
    grad_intents = gather(near, con.reshape(4 * CHIPS, BLK, width))
    return grad_utter.reshape(UBD * UB, width), grad_intents.reshape(BLK_DEV * BLK, width)


def solution(mesh):
    return jax.shard_map(
        shards,
        mesh=mesh,
        in_specs=(
            P(("dp", "cls"), "feat"),
            P(("dp", "cls"), "feat"),
            P(),
            P(),
            P(),
            P(("dp", "cls"), None),
        ),
        out_specs=(P(("dp", "cls"), "feat"), P(("dp", "cls"), "feat")),
        check_vma=False,
    )
```

```python
import jax
import jax.numpy as jnp
import numpy as np
from jax import lax
from jax.experimental import pallas as pl
from jax.experimental.pallas import tpu as pltpu
from jax.sharding import PartitionSpec as P

BLK = 128
BLK_DEV = 64
UB = 128
UBD = 8
MOST = 16
GAMMA = 4.0
MARGIN = 0.25

NY, NZ = 4, 8
CHIPS = NY * NZ
SLOTS = 4
DEPTH = 8
CON_DEPTH = 4
LAG_SLOPE = 2
LAG_GRAD = 4
PARTS = 2
PART = UBD // PARTS
ROWS = 32
MESH = pl.DeviceIdType.MESH

NODES = (
    (0, 0, -1, -1, 1),
    (1, 0, 0, 2, 1),
    (0, 1, 0, 0, 1),
    (0, 7, 0, 1, 0),
    (2, 0, 1, 2, 1),
    (0, 2, 2, 0, 1),
    (3, 1, 2, 3, 0),
    (3, 0, 4, 2, 0),
    (2, 7, 4, 1, 1),
    (2, 1, 4, 0, 0),
    (1, 2, 5, 2, 1),
    (0, 3, 5, 0, 1),
    (3, 2, 5, 3, 0),
    (1, 7, 8, 3, 0),
    (2, 6, 8, 1, 1),
    (3, 3, 11, 3, 1),
    (1, 1, 10, 1, 0),
    (0, 4, 11, 0, 1),
    (1, 6, 14, 3, 0),
    (3, 6, 14, 2, 0),
    (2, 3, 15, 3, 1),
    (2, 5, 14, 1, 0),
    (0, 5, 17, 0, 1),
    (2, 2, 20, 1, 0),
    (2, 4, 20, 0, 0),
    (3, 5, 22, 3, 0),
    (1, 5, 22, 2, 0),
    (0, 6, 22, 0, 0),
    (3, 4, 15, 0, 0),
    (1, 4, 17, 2, 0),
    (1, 3, 20, 3, 0),
    (3, 7, 8, 2, 0),
)
TASKS = (
    (("A", 0, 0), ("A", 0, 1),),
    (("A", 1, 0), ("A", 2, 0), ("A", 1, 1), ("A", 2, 1),),
    (),
    (("A", 4, 0),),
    (("A", 4, 1),),
    (("A", 5, 0), ("A", 5, 1),),
    (),
    (("A", 8, 0),),
    (("A", 8, 1), ("A", 10, 0),),
    (("A", 10, 1),),
    (("A", 11, 0),),
    (("A", 11, 1),),
    (("A", 14, 0),),
    (("A", 15, 0),),
    (("A", 14, 1),),
    (("A", 17, 0), ("A", 15, 1),),
    (),
    (("A", 17, 1), ("A", 20, 0),),
    (),
    (),
    (("A", 22, 0), ("A", 20, 1),),
    (),
    (("A", 22, 1),),
    (),
    (),
    (("R", 10, 0), ("R", 10, 1),),
    (),
    (),
    (("R", 14, 0), ("R", 14, 1),),
    (),
    (),
    (),
    (),
    (),
    (("R", 22, 0), ("R", 22, 1),),
    (),
)
LAST = (("R", 17, 0), ("R", 20, 0), ("R", 20, 1), ("R", 17, 1), ("R", 8, 0), ("R", 8, 1), ("R", 15, 0), ("R", 15, 1), ("R", 4, 0), ("R", 11, 0), ("R", 4, 1), ("R", 11, 1), ("R", 5, 0), ("R", 1, 0), ("R", 5, 1), ("R", 1, 1), ("R", 2, 0), ("R", 2, 1), ("R", 0, 0), ("R", 0, 1),)

DIRS = ((0, 1), (0, -1), (1, 0), (-1, 0))
INNER = [k for k in range(CHIPS) if NODES[k][4]]
OUTER = [k for k in range(CHIPS) if not NODES[k][4]]
SPOT = {k: i for i, k in enumerate(INNER)}
SPOT.update({k: i for i, k in enumerate(OUTER)})
KIDS = {k: [c for c in range(CHIPS) if NODES[c][2] == k] for k in range(CHIPS)}


def _sources():
    rows = np.zeros((CHIPS, 2, 3 * CHIPS), np.int32)
    goal = np.zeros((CHIPS, 2, 3 * CHIPS), np.int32)
    for y in range(NY):
        for z in range(NZ):
            for core in range(2):
                out, aim = [], []
                for c in range(2):
                    sign = 1 - 2 * c
                    for dy, dz, *_ in NODES:
                        out.append((z - sign * dz) % NZ * 2 * NY + (y - sign * dy) % NY * 2 + c)
                        aim.append(z * NY + y)
                sign = 1 - 2 * core
                for dy, dz, parent, way, _ in NODES:
                    step = DIRS[way] if parent >= 0 else (0, 0)
                    py, pz = y + sign * step[0], z + sign * step[1]
                    out.append((pz - sign * dz) % NZ * 2 * NY + (py - sign * dy) % NY * 2 + core)
                    aim.append(pz % NZ * NY + py % NY)
                rows[y * NZ + z, core], goal[y * NZ + z, core] = out, aim
    return rows, goal


SOURCE, GOAL = _sources()


def tree_kernel(
    ku_ref, lb_ref, bid_ref, scale_ref, kid_ref, utter_ref, lab_ref, intents_ref,
    gu_ref, con_ref,
    ag, outer, stage, aglab, rsin, rep, w, ucur, usel, labsel, part, recv, gs, gown, gbuf, cst,
    sem_in, sem_w, ag_send, ag_recv, out_send, out_recv, lab_send, lab_recv, rs_send, rs_recv, rep_send, rep_recv,
    part_send, part_recv, gs_send, gs_recv, con_send, con_recv, con_loc, sem_out,
):
    z = lax.axis_index("dp")
    cl = lax.axis_index("cls")
    x = lax.axis_index("feat")
    y = cl // 2
    core = cl % 2
    sign = 1 - 2 * core

    def toward(way, back=False):
        dy, dz = DIRS[way]
        flip = -sign if back else sign
        return ((z + NZ + flip * dz) % NZ, (y + NY + flip * dy) % NY * 2 + core, x)

    other = (z, y * 2 + (1 - core), x)

    def peer(o):
        return (z, cl, (x + o) % 4)

    def remote(src, dst, send, recv_sem, device):
        return pltpu.make_async_remote_copy(
            src_ref=src, dst_ref=dst, send_sem=send, recv_sem=recv_sem, device_id=device, device_id_type=MESH)

    def ag_copy(k, h):
        piece = pl.ds(h * PART, PART)
        return remote(ag.at[SPOT[NODES[k][2]], piece], ag.at[SPOT[k], piece],
                      ag_send.at[SPOT[k], h], ag_recv.at[SPOT[k], h], toward(NODES[k][3]))

    def out_copy(k):
        return remote(stage.at[SPOT[k]], outer.at[SPOT[k]], out_send.at[SPOT[k]], out_recv.at[SPOT[k]], toward(NODES[k][3]))

    def lab_copy(k):
        return remote(aglab.at[NODES[k][2]], aglab.at[k], lab_send.at[k], lab_recv.at[k], toward(NODES[k][3]))

    def rs_copy(k, h):
        piece = pl.ds(h * PART, PART)
        return remote(ag.at[SPOT[k], piece], rsin.at[SPOT[k], piece],
                      rs_send.at[SPOT[k], h], rs_recv.at[SPOT[k], h], toward(NODES[k][3], True))

    def rep_copy(k):
        return remote(outer.at[SPOT[k]], rep.at[SPOT[k]], rep_send.at[SPOT[k]], rep_recv.at[SPOT[k]], toward(NODES[k][3], True))

    def part_copy(n, o):
        return remote(part.at[n % DEPTH, (x + o) % 4], recv.at[n % DEPTH, o - 1],
                      part_send.at[n % DEPTH, o - 1], part_recv.at[n % DEPTH, o - 1], peer(o))

    def gs_copy(m, o):
        return remote(gs.at[m % DEPTH, x], gs.at[m % DEPTH, x],
                      gs_send.at[m % DEPTH, o - 1], gs_recv.at[m % DEPTH, o - 1], peer(o))

    def gs_wait(m, o):
        place = gs.at[m % DEPTH, (x + 4 - o) % 4]
        remote(place, place, gs_send.at[m % DEPTH, o - 1], gs_recv.at[m % DEPTH, o - 1], peer(o)).wait_recv()

    def con_far(m):
        return remote(cst.at[m % CON_DEPTH, pl.ds(2 * (1 - core), 2)], con_ref.at[core, m],
                      con_send.at[m % CON_DEPTH], con_recv.at[m], other)

    def con_far_wait(m):
        remote(cst.at[m % CON_DEPTH, pl.ds(2 * (1 - core), 2)], con_ref.at[1 - core, m],
               con_send.at[m % CON_DEPTH], con_recv.at[m], other).wait_recv()

    def con_near(m):
        return pltpu.make_async_copy(
            cst.at[m % CON_DEPTH, pl.ds(2 * core, 2)], con_ref.at[core, m], con_loc.at[m % CON_DEPTH])

    def out_dma(h):
        piece = pl.ds(h * PART, PART)
        return pltpu.make_async_copy(ag.at[0, piece], gu_ref.at[piece], sem_out.at[h])

    own_u = pltpu.make_async_copy(utter_ref, ag.at[0], sem_in.at[0])
    own_l = pltpu.make_async_copy(lab_ref, aglab.at[0], sem_in.at[1])
    own_w = pltpu.make_async_copy(intents_ref, w.at[pl.ds(core * BLK_DEV, BLK_DEV)], sem_in.at[2])
    far_w = remote(intents_ref, w.at[pl.ds(core * BLK_DEV, BLK_DEV)], sem_w.at[0], sem_w.at[1], other)
    far_w_in = remote(intents_ref, w.at[pl.ds((1 - core) * BLK_DEV, BLK_DEV)], sem_w.at[0], sem_w.at[1], other)
    own_u.start()
    own_l.start()
    own_w.start()

    barrier = pltpu.get_barrier_semaphore()
    for device in [toward(way) for way in range(4)] + [other, peer(1), peer(2), peer(3)]:
        pl.semaphore_signal(barrier, inc=1, device_id=device, device_id_type=MESH)
    pl.semaphore_wait(barrier, 8)
    own_u.wait()
    own_l.wait()
    far_w.start()

    def pass_on(k, h):
        if k > 0:
            ag_copy(k, h).wait_recv()
            if h == 0:
                lab_copy(k).wait_recv()
        for c in KIDS[k]:
            if NODES[c][4]:
                ag_copy(c, h).start()
                if h == 0:
                    lab_copy(c).start()

    def pick(k):
        d = k % DEPTH
        if NODES[k][4]:
            for j in range(UBD):
                ucur[j] = ag[SPOT[k], j]
            for c in KIDS[k]:
                if not NODES[c][4]:
                    for s in range(SLOTS):
                        stage[SPOT[c], s] = ucur[kid_ref[c * SLOTS + s]]
                    out_copy(c).start()
                    lab_copy(c).start()
            for s in range(SLOTS):
                usel[d, s] = ucur[ku_ref[k * SLOTS + s]]
        else:
            out_copy(k).wait_recv()
            lab_copy(k).wait_recv()
            for s in range(SLOTS):
                usel[d, s] = outer[SPOT[k], s]

    def scores(n):
        d = n % DEPTH

        @pl.when(n >= DEPTH)
        def _():
            for o in range(1, 4):
                part_copy(n, o).wait_send()

        mine = ku_ref[n * SLOTS + x]
        rows = lax.broadcasted_iota(jnp.int32, (UBD, UB), 0)
        for k in range(2):
            labs = aglab[n, k * UBD:(k + 1) * UBD]
            labsel[d, k:k + 1] = jnp.sum(jnp.where(rows == mine, labs, 0), axis=0, keepdims=True)
        for s in range(SLOTS):
            part[d, s] = lax.dot_general(
                w[lb_ref[n * SLOTS + s]], usel[d, s], (((1,), (1,)), ((), ())),
                preferred_element_type=jnp.float32).astype(part.dtype)
        for o in range(1, 4):
            part_copy(n, o).start()

    def slopes(m):
        d = m % DEPTH

        @pl.when(m >= DEPTH)
        def _():
            for o in range(1, 4):
                gs_copy(m, o).wait_send()

        total = part[d, x].astype(jnp.float32)
        for o in range(1, 4):
            part_copy(m, o).wait_recv()
            total = total + recv[d, o - 1].astype(jnp.float32)
        logits = GAMMA * total
        ids = lax.broadcasted_iota(jnp.int32, (BLK, UB), 0) + bid_ref[m * SLOTS + x] * BLK
        hit = (ids == labsel[d, 0:1]) | (ids == labsel[d, 1:2])
        slope = jax.nn.sigmoid(jnp.where(hit, MARGIN - logits, logits + MARGIN))
        slope = jnp.where(hit, -slope, slope) * scale_ref[m * SLOTS + x]
        gs[d, x] = slope.astype(jnp.bfloat16)
        for o in range(1, 4):
            gs_copy(m, o).start()

    def grads(m):
        d = m % DEPTH
        e = m % CON_DEPTH

        @pl.when(m >= CON_DEPTH)
        def _():
            con_far(m).wait_send()
            con_near(m).wait()

        for o in range(1, 4):
            gs_wait(m, o)
        for s in range(SLOTS):
            slope = gs[d, s]
            cst[e, s] = jnp.dot(slope, usel[d, s], preferred_element_type=jnp.float32).astype(jnp.bfloat16)
            gown[s] = lax.dot_general(
                slope, w[lb_ref[m * SLOTS + s]], (((0,), (0,)), ((), ())),
                preferred_element_type=jnp.float32)
        con_far(m).start()
        con_near(m).start()

    def keep(k):
        if NODES[k][4]:
            for s in range(SLOTS):
                gbuf[SPOT[k], s] = gown[s]
        else:
            for s in range(SLOTS):
                outer[SPOT[k], s] = gown[s].astype(jnp.bfloat16)
            rep_copy(k).start()

    def fold(k, h):
        inner = [c for c in KIDS[k] if NODES[c][4]]
        outer_kids = [c for c in KIDS[k] if not NODES[c][4]]
        for c in inner:
            rs_copy(c, h).wait_recv()
            ag_copy(c, h).wait_send()
        if h == 0:
            for c in outer_kids:
                rep_copy(c).wait_recv()
        tiles = UB // ROWS

        def tile(i, carry):
            j = h * PART + i // tiles
            rows = pl.ds(pl.multiple_of(i % tiles * ROWS, ROWS), ROWS)
            total = jnp.zeros((ROWS, ag.shape[3]), jnp.float32)
            for s in range(SLOTS):
                total = total + gbuf[SPOT[k], s, rows] * (ku_ref[k * SLOTS + s] == j).astype(jnp.float32)
            for c in outer_kids:
                for s in range(SLOTS):
                    share = (kid_ref[c * SLOTS + s] == j).astype(jnp.float32)
                    total = total + rep[SPOT[c], s, rows].astype(jnp.float32) * share
            for c in inner:
                total = total + rsin[SPOT[c], j, rows].astype(jnp.float32)
            ag[SPOT[k], j, rows] = total.astype(jnp.bfloat16)
            return carry

        lax.fori_loop(0, PART * tiles, tile, 0)
        if k == 0:
            out_dma(h).start()
        else:
            rs_copy(k, h).start()

    def do(tasks):
        for kind, k, h in tasks:
            if kind == "A":
                pass_on(k, h)
            else:
                fold(k, h)

    def step(n, carry):
        for k in range(len(TASKS)):
            if k < CHIPS or TASKS[k]:
                @pl.when(n == k)
                def _():
                    do(TASKS[k])
                    if k < CHIPS:
                        pick(k)
                    if k == 0:
                        own_w.wait()
                        far_w_in.wait_recv()

        @pl.when(n < CHIPS)
        def _():
            scores(n)

        @pl.when((n >= LAG_SLOPE) & (n < CHIPS + LAG_SLOPE))
        def _():
            slopes(n - LAG_SLOPE)

        @pl.when(n >= LAG_GRAD)
        def _():
            grads(n - LAG_GRAD)

        for k in range(CHIPS):
            @pl.when(n == k + LAG_GRAD)
            def _():
                keep(k)
        return carry

    lax.fori_loop(0, CHIPS + LAG_GRAD, step, 0)
    do(LAST)

    for k in range(1, CHIPS):
        lab_copy(k).wait_send()
        if NODES[k][4]:
            for h in range(PARTS):
                rs_copy(k, h).wait_send()
        else:
            out_copy(k).wait_send()
            rep_copy(k).wait_send()

    def drain(n, carry):
        con_far_wait(n)
        return carry

    lax.fori_loop(0, CHIPS, drain, 0)
    for n in range(CHIPS - DEPTH, CHIPS):
        for o in range(1, 4):
            part_copy(n, o).wait_send()
            gs_copy(n, o).wait_send()
    for n in range(CHIPS - CON_DEPTH, CHIPS):
        con_far(n).wait_send()
        con_near(n).wait()
    far_w.wait_send()
    for h in range(PARTS):
        out_dma(h).wait()


def tree(ku, lb, bid, scale, kid, utter, labs, intents):
    width = intents.shape[2]
    block = (UB, width)
    dma = pltpu.SemaphoreType.DMA
    anyspace = pl.BlockSpec(memory_space=pl.ANY)
    smem = pl.BlockSpec(memory_space=pltpu.SMEM)
    ni, no = len(INNER), len(OUTER)
    bf16 = jnp.bfloat16
    return pl.pallas_call(
        tree_kernel,
        out_shape=(
            jax.ShapeDtypeStruct((UBD,) + block, bf16),
            jax.ShapeDtypeStruct((2, CHIPS, 2) + block, bf16),
        ),
        in_specs=[smem] * 5 + [anyspace] * 3,
        out_specs=(anyspace, anyspace),
        scratch_shapes=[
            pltpu.VMEM((ni, UBD) + block, bf16),
            pltpu.VMEM((no, SLOTS) + block, bf16),
            pltpu.VMEM((no, SLOTS) + block, bf16),
            pltpu.VMEM((CHIPS, 2 * UBD, UB), jnp.int32),
            pltpu.VMEM((ni, UBD) + block, bf16),
            pltpu.VMEM((no, SLOTS) + block, bf16),
            pltpu.VMEM((2 * BLK_DEV,) + block, bf16),
            pltpu.VMEM((UBD,) + block, bf16),
            pltpu.VMEM((DEPTH, SLOTS) + block, bf16),
            pltpu.VMEM((DEPTH, 8, UB), jnp.int32),
            pltpu.VMEM((DEPTH, SLOTS, BLK, UB), SCORE),
            pltpu.VMEM((DEPTH, 3, BLK, UB), SCORE),
            pltpu.VMEM((DEPTH, SLOTS, BLK, UB), bf16),
            pltpu.VMEM((SLOTS,) + block, jnp.float32),
            pltpu.VMEM((ni, SLOTS) + block, jnp.float32),
            pltpu.VMEM((CON_DEPTH, SLOTS) + block, bf16),
            dma((3,)), dma((2,)),
            dma((ni, PARTS)), dma((ni, PARTS)), dma((no,)), dma((no,)), dma((CHIPS,)), dma((CHIPS,)),
            dma((ni, PARTS)), dma((ni, PARTS)), dma((no,)), dma((no,)),
            dma((DEPTH, 3)), dma((DEPTH, 3)), dma((DEPTH, 3)), dma((DEPTH, 3)),
            dma((CON_DEPTH,)), dma((CHIPS,)), dma((CON_DEPTH,)), dma((PARTS,)),
        ],
        compiler_params=pltpu.CompilerParams(
            collective_id=0, has_side_effects=True, vmem_limit_bytes=60 * 1024 * 1024),
        name="tree",
    )(ku, lb, bid, scale, kid, utter, labs, intents)


SCORE = jnp.bfloat16
CHUNK = 16


def gather_kernel(lb_ref, con_ref, out_ref, con, acc, res, sem_in, sem_out):
    count = con.shape[0]

    def load(i):
        piece = pl.ds(i * CHUNK, CHUNK)
        return pltpu.make_async_copy(con_ref.at[piece], con.at[piece], sem_in.at[i])

    def store(i):
        piece = pl.ds(i * CHUNK, CHUNK)
        return pltpu.make_async_copy(res.at[piece], out_ref.at[piece], sem_out.at[i])

    for i in range(count // CHUNK):
        load(i).start()
    acc[...] = jnp.zeros_like(acc)
    for i in range(count // CHUNK):
        load(i).wait()

        def add(k, carry):
            b = lb_ref[i * CHUNK + k]
            acc[b] = acc[b] + con[i * CHUNK + k].astype(jnp.float32)
            return carry

        lax.fori_loop(0, CHUNK, add, 0)
    for i in range(BLK_DEV // CHUNK):
        piece = pl.ds(i * CHUNK, CHUNK)
        res[piece] = acc[piece].astype(res.dtype)
        store(i).start()
    for i in range(BLK_DEV // CHUNK):
        store(i).wait()


def gather(lb, con):
    count, width = con.shape[0], con.shape[2]
    dma = pltpu.SemaphoreType.DMA
    return pl.pallas_call(
        gather_kernel,
        in_specs=[pl.BlockSpec(memory_space=pltpu.SMEM), pl.BlockSpec(memory_space=pl.ANY)],
        out_specs=pl.BlockSpec(memory_space=pl.ANY),
        scratch_shapes=[
            pltpu.VMEM((count, BLK, width), jnp.bfloat16),
            pltpu.VMEM((BLK_DEV, BLK, width), jnp.float32),
            pltpu.VMEM((BLK_DEV, BLK, width), jnp.bfloat16),
            dma((count // CHUNK,)), dma((BLK_DEV // CHUNK,)),
        ],
        out_shape=jax.ShapeDtypeStruct((BLK_DEV, BLK, width), jnp.bfloat16),
        compiler_params=pltpu.CompilerParams(vmem_limit_bytes=60 * 1024 * 1024),
        name="sum_blocks",
    )(lb, con)


def plan(req_blocks, req_count, block_home):
    z = lax.axis_index("dp")
    cl = lax.axis_index("cls")
    chip, core = (cl // 2) * NZ + z, cl % 2
    rows = lax.dynamic_slice(jnp.asarray(SOURCE), (chip, core, 0), (1, 1, 3 * CHIPS)).reshape(3 * CHIPS)
    goal = lax.dynamic_slice(jnp.asarray(GOAL), (chip, core, 0), (1, 1, 3 * CHIPS)).reshape(3 * CHIPS)
    entries = UBD * MOST
    wide = 64
    req = req_blocks.reshape(2 * CHIPS * entries)
    spread = (jnp.arange(wide)[:, None] == (req // wide)[None, :]).astype(jnp.bfloat16)
    table = block_home.reshape(wide, wide).T
    halves = jnp.concatenate([table // wide, table % wide], axis=0).astype(jnp.bfloat16)
    found = jnp.dot(halves, spread, preferred_element_type=jnp.float32).reshape(2, wide, -1)
    low = jnp.arange(wide)[:, None] == (req % wide)[None, :]
    found = jnp.sum(jnp.where(low[None], found, 0.0), axis=1).astype(jnp.int32)
    home = jnp.where(req >= 0, found[0] * wide + found[1], -1)
    req = req.reshape(2 * CHIPS, entries)[rows]
    home = home.reshape(2 * CHIPS, entries)[rows]
    count = req_count.reshape(2 * CHIPS, UBD)[rows]
    at = jnp.arange(entries)[None, None, :]
    side = goal[:, None] * 2 + jnp.arange(2)[None, :]
    mine = (home[:, None, :] >= 0) & (home[:, None, :] // BLK_DEV == side[:, :, None])
    first = jnp.min(jnp.where(mine, at, entries), axis=2)
    last = jnp.max(jnp.where(mine, at, -1), axis=2)
    entry = jnp.stack([first, last], axis=2)
    valid = jnp.stack([last >= 0, last > first], axis=2)
    hot = (at[..., None, :] == entry[..., None]) & valid[..., None]
    lb = jnp.sum(jnp.where(hot, home[:, None, None, :] % (2 * BLK_DEV), 0), axis=3)
    bid = jnp.sum(jnp.where(hot, req[:, None, None, :], 0), axis=3)
    ku = jnp.where(valid, entry // MOST, 0)
    listed = jnp.sum(jnp.where(ku[..., None] == jnp.arange(UBD), count[:, None, None, :], 0), axis=3)
    scale = jnp.where(valid, GAMMA / listed.astype(jnp.float32), 0.0)
    return ku, lb, bid, scale


def shards(utter, intents, req_blocks, req_count, block_home, labels):
    core = lax.axis_index("cls") % 2
    width = intents.shape[1]
    ku, lb, bid, scale = plan(req_blocks, req_count, block_home)

    def row(t, c):
        return lax.dynamic_slice_in_dim(t.reshape(3 * CHIPS * SLOTS), c * CHIPS * SLOTS, CHIPS * SLOTS)

    labs = labels.reshape(UBD, UB, 2).transpose(2, 0, 1).reshape(2 * UBD, UB)
    grad_utter, con = tree(
        row(ku, core), row(lb, core), row(bid, core), row(scale, core), row(ku, 2),
        utter.reshape(UBD, UB, width), labs, intents.reshape(BLK_DEV, BLK, width))
    near = lax.dynamic_index_in_dim(
        lb[:2 * CHIPS].reshape(2 * CHIPS, 2, 2), core, 1, keepdims=False).reshape(4 * CHIPS) % BLK_DEV
    grad_intents = gather(near, con.reshape(4 * CHIPS, BLK, width))
    return grad_utter.reshape(UBD * UB, width), grad_intents.reshape(BLK_DEV * BLK, width)


def solution(mesh):
    return jax.shard_map(
        shards,
        mesh=mesh,
        in_specs=(
            P(("dp", "cls"), "feat"),
            P(("dp", "cls"), "feat"),
            P(),
            P(),
            P(),
            P(("dp", "cls"), None),
        ),
        out_specs=(P(("dp", "cls"), "feat"), P(("dp", "cls"), "feat")),
        check_vma=False,
    )
```

```python
import jax
import jax.numpy as jnp
from jax import lax
from jax.experimental import pallas as pl
from jax.experimental.pallas import tpu as pltpu
from jax.sharding import PartitionSpec as P

BLK = 128
BLK_DEV = 64
UB = 128
UBD = 8
MOST = 16
GAMMA = 4.0
MARGIN = 0.25

NY, NZ = 4, 8
CHIPS = NY * NZ
SLOTS = 4
DEPTH = 8
CON_DEPTH = 4
LAG_SLOPE = 2
LAG_GRAD = 4
PARTS = 2
PART = UBD // PARTS
ROWS = 32
MESH = pl.DeviceIdType.MESH

NODES = (
    (0, 0, -1, -1, 1),
    (1, 0, 0, 2, 1),
    (0, 1, 0, 0, 1),
    (0, 7, 0, 1, 1),
    (2, 0, 1, 2, 1),
    (3, 1, 2, 3, 0),
    (0, 2, 2, 0, 1),
    (1, 1, 2, 2, 0),
    (1, 7, 3, 2, 0),
    (2, 7, 4, 1, 1),
    (0, 6, 3, 1, 0),
    (3, 2, 6, 3, 0),
    (0, 3, 6, 0, 1),
    (3, 7, 3, 3, 0),
    (2, 6, 9, 1, 1),
    (1, 3, 12, 2, 1),
    (2, 1, 4, 0, 0),
    (0, 4, 12, 0, 1),
    (2, 5, 14, 1, 0),
    (1, 6, 14, 3, 0),
    (3, 6, 14, 2, 0),
    (2, 3, 15, 2, 1),
    (1, 2, 15, 1, 0),
    (3, 4, 17, 3, 0),
    (2, 4, 21, 0, 0),
    (0, 5, 17, 0, 1),
    (2, 2, 21, 1, 0),
    (3, 3, 21, 2, 0),
    (1, 5, 25, 2, 0),
    (3, 5, 25, 3, 0),
    (1, 4, 15, 0, 0),
    (3, 0, 4, 2, 0),
)
TASKS = (
    (("A", 0, 0), ("A", 0, 1),),
    (("A", 2, 0), ("A", 1, 0), ("A", 3, 0), ("A", 1, 1),),
    (("A", 2, 1),),
    (("A", 4, 0), ("A", 3, 1),),
    (("A", 4, 1),),
    (("A", 6, 0),),
    (("A", 6, 1),),
    (("A", 9, 0),),
    (),
    (("A", 9, 1),),
    (),
    (("A", 12, 0),),
    (("A", 12, 1),),
    (("A", 15, 0), ("A", 14, 0),),
    (("A", 14, 1),),
    (("A", 15, 1),),
    (("A", 17, 0),),
    (("A", 17, 1),),
    (("A", 21, 0),),
    (),
    (),
    (("A", 21, 1),),
    (("A", 25, 0),),
    (("A", 25, 1),),
    (("R", 3, 0), ("R", 3, 1),),
    (),
    (),
    (),
    (("R", 14, 0), ("R", 14, 1),),
    (),
    (),
    (("R", 9, 0),),
    (("R", 9, 1),),
    (),
    (("R", 21, 0), ("R", 21, 1),),
    (),
)
LAST = (("R", 25, 0), ("R", 25, 1), ("R", 15, 0), ("R", 17, 0), ("R", 15, 1), ("R", 17, 1), ("R", 4, 0), ("R", 4, 1), ("R", 12, 0), ("R", 12, 1), ("R", 6, 0), ("R", 1, 0), ("R", 6, 1), ("R", 1, 1), ("R", 2, 0), ("R", 2, 1), ("R", 0, 0), ("R", 0, 1),)

DIRS = ((0, 1), (0, -1), (1, 0), (-1, 0))
INNER = [k for k in range(CHIPS) if NODES[k][4]]
OUTER = [k for k in range(CHIPS) if not NODES[k][4]]
SPOT = {k: i for i, k in enumerate(INNER)}
SPOT.update({k: i for i, k in enumerate(OUTER)})
KIDS = {k: [c for c in range(CHIPS) if NODES[c][2] == k] for k in range(CHIPS)}


def tree_kernel(
    req_ref, home_ref, lab_ref, utter_ref, intents_ref,
    gu_ref, con_ref, tabs_ref,
    ag, outer, stage, aglab, rsin, rep, w, ucur, usel, labsel, part, recv, gs, gown, gbuf, cst, reqs, homes, tab, rows_ref,
    sem_in, sem_w, ag_send, ag_recv, out_send, out_recv, lab_send, lab_recv, rs_send, rs_recv, rep_send, rep_recv,
    part_send, part_recv, gs_send, gs_recv, con_send, con_recv, con_loc, sem_out, sem_tab,
):
    z = lax.axis_index("dp")
    cl = lax.axis_index("cls")
    x = lax.axis_index("feat")
    y = cl // 2
    core = cl % 2
    sign = 1 - 2 * core

    def toward(way, back=False):
        dy, dz = DIRS[way]
        flip = -sign if back else sign
        return ((z + NZ + flip * dz) % NZ, (y + NY + flip * dy) % NY * 2 + core, x)

    other = (z, y * 2 + (1 - core), x)

    def peer(o):
        return (z, cl, (x + o) % 4)

    def remote(src, dst, send, recv_sem, device):
        return pltpu.make_async_remote_copy(
            src_ref=src, dst_ref=dst, send_sem=send, recv_sem=recv_sem, device_id=device, device_id_type=MESH)

    def ag_copy(k, h):
        piece = pl.ds(h * PART, PART)
        return remote(ag.at[SPOT[NODES[k][2]], piece], ag.at[SPOT[k], piece],
                      ag_send.at[SPOT[k], h], ag_recv.at[SPOT[k], h], toward(NODES[k][3]))

    def out_copy(k):
        return remote(stage.at[SPOT[k]], outer.at[SPOT[k]], out_send.at[SPOT[k]], out_recv.at[SPOT[k]], toward(NODES[k][3]))

    def lab_copy(k):
        return remote(aglab.at[NODES[k][2]], aglab.at[k], lab_send.at[k], lab_recv.at[k], toward(NODES[k][3]))

    def rs_copy(k, h):
        piece = pl.ds(h * PART, PART)
        return remote(ag.at[SPOT[k], piece], rsin.at[SPOT[k], piece],
                      rs_send.at[SPOT[k], h], rs_recv.at[SPOT[k], h], toward(NODES[k][3], True))

    def rep_copy(k):
        return remote(outer.at[SPOT[k]], rep.at[SPOT[k]], rep_send.at[SPOT[k]], rep_recv.at[SPOT[k]], toward(NODES[k][3], True))

    def part_copy(n, o):
        return remote(part.at[n % DEPTH, (x + o) % 4], recv.at[n % DEPTH, o - 1],
                      part_send.at[n % DEPTH, o - 1], part_recv.at[n % DEPTH, o - 1], peer(o))

    def gs_copy(m, o):
        return remote(gs.at[m % DEPTH, x], gs.at[m % DEPTH, x],
                      gs_send.at[m % DEPTH, o - 1], gs_recv.at[m % DEPTH, o - 1], peer(o))

    def gs_wait(m, o):
        place = gs.at[m % DEPTH, (x + 4 - o) % 4]
        remote(place, place, gs_send.at[m % DEPTH, o - 1], gs_recv.at[m % DEPTH, o - 1], peer(o)).wait_recv()

    def con_far(m):
        return remote(cst.at[m % CON_DEPTH, pl.ds(2 * (1 - core), 2)], con_ref.at[core, m],
                      con_send.at[m % CON_DEPTH], con_recv.at[m], other)

    def con_far_wait(m):
        remote(cst.at[m % CON_DEPTH, pl.ds(2 * (1 - core), 2)], con_ref.at[1 - core, m],
               con_send.at[m % CON_DEPTH], con_recv.at[m], other).wait_recv()

    def con_near(m):
        return pltpu.make_async_copy(
            cst.at[m % CON_DEPTH, pl.ds(2 * core, 2)], con_ref.at[core, m], con_loc.at[m % CON_DEPTH])

    def out_dma(h):
        piece = pl.ds(h * PART, PART)
        return pltpu.make_async_copy(ag.at[0, piece], gu_ref.at[piece], sem_out.at[h])

    own_u = pltpu.make_async_copy(utter_ref, ag.at[0], sem_in.at[0])
    own_w = pltpu.make_async_copy(intents_ref, w.at[pl.ds(core * BLK_DEV, BLK_DEV)], sem_in.at[2])
    far_w = remote(intents_ref, w.at[pl.ds(core * BLK_DEV, BLK_DEV)], sem_w.at[0], sem_w.at[1], other)
    far_w_in = remote(intents_ref, w.at[pl.ds((1 - core) * BLK_DEV, BLK_DEV)], sem_w.at[0], sem_w.at[1], other)
    own_u.start()
    own_w.start()

    barrier = pltpu.get_barrier_semaphore()
    for device in [toward(way) for way in range(4)] + [other, peer(1), peer(2), peer(3)]:
        pl.semaphore_signal(barrier, inc=1, device_id=device, device_id_type=MESH)
    pl.semaphore_wait(barrier, 8)
    own_u.wait()
    for k in range(2):
        for i in range(UBD):
            aglab[0, k * UBD + i:k * UBD + i + 1] = lab_ref[k:k + 1, i * UB:(i + 1) * UB]
    far_w.start()

    tab_near = pltpu.make_async_copy(tab.at[pl.ds(0, CHIPS)], tabs_ref.at[core], sem_tab.at[1])
    tab_far = remote(tab.at[pl.ds(0, CHIPS)], tabs_ref.at[core], sem_tab.at[2], sem_tab.at[3], other)
    tab_in = remote(tab.at[pl.ds(0, CHIPS)], tabs_ref.at[1 - core], sem_tab.at[2], sem_tab.at[3], other)

    def pass_on(k, h):
        if k > 0:
            ag_copy(k, h).wait_recv()
            if h == 0:
                lab_copy(k).wait_recv()
        for c in KIDS[k]:
            if NODES[c][4]:
                ag_copy(c, h).start()
                if h == 0:
                    lab_copy(c).start()

    def pick(k):
        d = k % DEPTH
        if NODES[k][4]:
            for j in range(UBD):
                ucur[j] = ag[SPOT[k], j]
            for c in KIDS[k]:
                if not NODES[c][4]:
                    for s in range(SLOTS):
                        stage[SPOT[c], s] = ucur[block_of(CHIPS + c, s)]
                    out_copy(c).start()
                    lab_copy(c).start()
            for s in range(SLOTS):
                usel[d, s] = ucur[block_of(k, s)]
        else:
            out_copy(k).wait_recv()
            lab_copy(k).wait_recv()
            for s in range(SLOTS):
                usel[d, s] = outer[SPOT[k], s]

    def block_of(k, s):
        return rows_ref[k, s] % 8

    def place_of(k, s):
        return rows_ref[k, s] // 8 % 128

    def make_plan():
        lanes = 128
        for k in range(CHIPS):
            dy, dz = NODES[k][:2]
            row = (z + NZ - sign * dz) % NZ * 2 * NY + (y + NY - sign * dy) % NY * 2 + core
            reqs[k:k + 1] = req_ref[pl.ds(row, 1)]
        table = home_ref[...]
        high = (table // 64).astype(jnp.float32).astype(jnp.bfloat16)
        low = (table % 64).astype(jnp.float32).astype(jnp.bfloat16)
        tall = lax.broadcasted_iota(jnp.int32, (lanes, lanes), 0)
        for k in range(CHIPS):
            ids = reqs[k:k + 1]
            pick_hi = (tall[:32] == ids // lanes).astype(jnp.float32).astype(jnp.bfloat16)
            pick_lo = tall == ids % lanes
            contract = (((0,), (0,)), ((), ()))
            a = lax.dot_general(high, pick_hi, contract, preferred_element_type=jnp.float32)
            b = lax.dot_general(low, pick_hi, contract, preferred_element_type=jnp.float32)
            home = jnp.sum(jnp.where(pick_lo, a * 64.0 + b, 0.0), axis=0, keepdims=True)
            homes[k:k + 1] = jnp.where(ids >= 0, home.astype(jnp.int32), -1)
        here = z * NY + y
        codes = []
        for dy, dz in DIRS:
            codes.append((z + NZ + sign * dz) % NZ * NY + (y + NY + sign * dy) % NY)
        for k in range(CHIPS):
            parent, way = NODES[k][2:4]
            if parent >= 0:
                homes[CHIPS + k:CHIPS + k + 1] = homes[parent:parent + 1] + (here - codes[way]) * 2 * BLK_DEV
                reqs[CHIPS + k:CHIPS + k + 1] = reqs[parent:parent + 1]
            else:
                homes[CHIPS + k:CHIPS + k + 1] = jnp.full((1, lanes), -1, jnp.int32)
                reqs[CHIPS + k:CHIPS + k + 1] = jnp.full((1, lanes), -1, jnp.int32)
        ids, home = reqs[...], homes[...]
        lane = lax.broadcasted_iota(jnp.int32, ids.shape, 1)
        at = lane.astype(jnp.float32)
        packed = jnp.zeros(ids.shape, jnp.int32)

        def total(v):
            return jnp.sum(v.astype(jnp.float32), axis=1, keepdims=True).astype(jnp.int32)

        for o in range(2):
            base = here * 2 * BLK_DEV + o * BLK_DEV
            mine = (ids >= 0) & (home >= base) & (home < base + BLK_DEV)
            first = jnp.min(jnp.where(mine, at, 1000.0), axis=1, keepdims=True).astype(jnp.int32)
            last = jnp.max(jnp.where(mine, at, -1.0), axis=1, keepdims=True).astype(jnp.int32)
            for s, (entry, valid) in enumerate(((first, last >= 0), (last, last > first))):
                hot = mine & (lane == entry)
                block = entry // MOST
                place = total(jnp.where(hot, home - here * 2 * BLK_DEV, 0))
                name = total(jnp.where(hot, ids, 0))
                listed = total(jnp.where((ids >= 0) & (lane // MOST == block), 1, 0))
                value = block + 8 * place + 1024 * listed + 32768 * name
                value = jnp.where(valid, value, 0)
                packed = packed + jnp.where(lane == 2 * o + s, value, 0)
        tab[...] = packed
        fill = pltpu.make_async_copy(tab, rows_ref, sem_tab.at[0])
        fill.start()
        tab_near.start()
        tab_far.start()
        fill.wait()

    def scores(n):
        d = n % DEPTH

        @pl.when(n >= DEPTH)
        def _():
            for o in range(1, 4):
                part_copy(n, o).wait_send()

        mine = block_of(n, x)
        rows = lax.broadcasted_iota(jnp.int32, (UBD, UB), 0)
        for k in range(2):
            labs = aglab[n, k * UBD:(k + 1) * UBD]
            labsel[d, k:k + 1] = jnp.sum(jnp.where(rows == mine, labs, 0), axis=0, keepdims=True)
        for s in range(SLOTS):
            part[d, s] = lax.dot_general(
                w[place_of(n, s)], usel[d, s], (((1,), (1,)), ((), ())),
                preferred_element_type=jnp.float32).astype(part.dtype)
        for o in range(1, 4):
            part_copy(n, o).start()

    def slopes(m):
        d = m % DEPTH

        @pl.when(m >= DEPTH)
        def _():
            for o in range(1, 4):
                gs_copy(m, o).wait_send()

        total = part[d, x].astype(jnp.float32)
        for o in range(1, 4):
            part_copy(m, o).wait_recv()
            total = total + recv[d, o - 1].astype(jnp.float32)
        logits = GAMMA * total
        ids = lax.broadcasted_iota(jnp.int32, (BLK, UB), 0) + (rows_ref[m, x] // 32768) * BLK
        hit = (ids == labsel[d, 0:1]) | (ids == labsel[d, 1:2])
        slope = jax.nn.sigmoid(jnp.where(hit, MARGIN - logits, logits + MARGIN))
        listed = jnp.full((1, UB), rows_ref[m, x] // 1024 % 32, jnp.int32).astype(jnp.float32)
        scale = jnp.where(listed > 0, GAMMA / jnp.maximum(listed, 1.0), 0.0)
        slope = jnp.where(hit, -slope, slope) * scale
        gs[d, x] = slope.astype(jnp.bfloat16)
        for o in range(1, 4):
            gs_copy(m, o).start()

    def grads(m):
        d = m % DEPTH
        e = m % CON_DEPTH

        @pl.when(m >= CON_DEPTH)
        def _():
            con_far(m).wait_send()
            con_near(m).wait()

        for o in range(1, 4):
            gs_wait(m, o)
        for s in range(SLOTS):
            slope = gs[d, s]
            cst[e, s] = jnp.dot(slope, usel[d, s], preferred_element_type=jnp.float32).astype(jnp.bfloat16)
            gown[s] = lax.dot_general(
                slope, w[place_of(m, s)], (((0,), (0,)), ((), ())),
                preferred_element_type=jnp.float32)
        con_far(m).start()
        con_near(m).start()

    def keep(k):
        if NODES[k][4]:
            for s in range(SLOTS):
                gbuf[SPOT[k], s] = gown[s]
        else:
            for s in range(SLOTS):
                outer[SPOT[k], s] = gown[s].astype(jnp.bfloat16)
            rep_copy(k).start()

    def fold(k, h):
        inner = [c for c in KIDS[k] if NODES[c][4]]
        outer_kids = [c for c in KIDS[k] if not NODES[c][4]]
        for c in inner:
            rs_copy(c, h).wait_recv()
            ag_copy(c, h).wait_send()
        if h == 0:
            for c in outer_kids:
                rep_copy(c).wait_recv()
        tiles = UB // ROWS

        def tile(i, carry):
            j = h * PART + i // tiles
            rows = pl.ds(pl.multiple_of(i % tiles * ROWS, ROWS), ROWS)
            total = jnp.zeros((ROWS, ag.shape[3]), jnp.float32)
            for s in range(SLOTS):
                total = total + gbuf[SPOT[k], s, rows] * (block_of(k, s) == j).astype(jnp.float32)
            for c in outer_kids:
                for s in range(SLOTS):
                    share = (block_of(CHIPS + c, s) == j).astype(jnp.float32)
                    total = total + rep[SPOT[c], s, rows].astype(jnp.float32) * share
            for c in inner:
                total = total + rsin[SPOT[c], j, rows].astype(jnp.float32)
            ag[SPOT[k], j, rows] = total.astype(jnp.bfloat16)
            return carry

        lax.fori_loop(0, PART * tiles, tile, 0)
        if k == 0:
            out_dma(h).start()
        else:
            rs_copy(k, h).start()

    def do(tasks):
        for kind, k, h in tasks:
            if kind == "A":
                pass_on(k, h)
            else:
                fold(k, h)

    def step(n, carry):
        for k in range(len(TASKS)):
            if k < CHIPS or TASKS[k]:
                @pl.when(n == k)
                def _():
                    if k > 0:
                        do(TASKS[k])
                    if k < CHIPS:
                        pick(k)
                    if k == 0:
                        own_w.wait()
                        far_w_in.wait_recv()

        @pl.when(n < CHIPS)
        def _():
            scores(n)

        @pl.when((n >= LAG_SLOPE) & (n < CHIPS + LAG_SLOPE))
        def _():
            slopes(n - LAG_SLOPE)

        @pl.when(n >= LAG_GRAD)
        def _():
            grads(n - LAG_GRAD)

        for k in range(CHIPS):
            @pl.when(n == k + LAG_GRAD)
            def _():
                keep(k)
        return carry

    do(TASKS[0])
    make_plan()
    lax.fori_loop(0, CHIPS + LAG_GRAD, step, 0)
    do(LAST)

    for k in range(1, CHIPS):
        lab_copy(k).wait_send()
        if NODES[k][4]:
            for h in range(PARTS):
                rs_copy(k, h).wait_send()
        else:
            out_copy(k).wait_send()
            rep_copy(k).wait_send()

    def drain(n, carry):
        con_far_wait(n)
        return carry

    lax.fori_loop(0, CHIPS, drain, 0)
    for n in range(CHIPS - DEPTH, CHIPS):
        for o in range(1, 4):
            part_copy(n, o).wait_send()
            gs_copy(n, o).wait_send()
    for n in range(CHIPS - CON_DEPTH, CHIPS):
        con_far(n).wait_send()
        con_near(n).wait()
    far_w.wait_send()
    tab_near.wait()
    tab_far.wait_send()
    tab_in.wait_recv()
    for h in range(PARTS):
        out_dma(h).wait()


def tree(req, home, labs, utter, intents):
    width = intents.shape[2]
    block = (UB, width)
    dma = pltpu.SemaphoreType.DMA
    anyspace = pl.BlockSpec(memory_space=pl.ANY)
    vmem = pl.BlockSpec(memory_space=pltpu.VMEM)
    ni, no = len(INNER), len(OUTER)
    bf16 = jnp.bfloat16
    return pl.pallas_call(
        tree_kernel,
        out_shape=(
            jax.ShapeDtypeStruct((UBD,) + block, bf16),
            jax.ShapeDtypeStruct((2, CHIPS, 2) + block, bf16),
            jax.ShapeDtypeStruct((2, CHIPS, 128), jnp.int32),
        ),
        in_specs=[vmem] * 3 + [anyspace] * 2,
        out_specs=(anyspace, anyspace, anyspace),
        scratch_shapes=[
            pltpu.VMEM((ni, UBD) + block, bf16),
            pltpu.VMEM((no, SLOTS) + block, bf16),
            pltpu.VMEM((no, SLOTS) + block, bf16),
            pltpu.VMEM((CHIPS, 2 * UBD, UB), jnp.int32),
            pltpu.VMEM((ni, UBD) + block, bf16),
            pltpu.VMEM((no, SLOTS) + block, bf16),
            pltpu.VMEM((2 * BLK_DEV,) + block, bf16),
            pltpu.VMEM((UBD,) + block, bf16),
            pltpu.VMEM((DEPTH, SLOTS) + block, bf16),
            pltpu.VMEM((DEPTH, 8, UB), jnp.int32),
            pltpu.VMEM((DEPTH, SLOTS, BLK, UB), SCORE),
            pltpu.VMEM((DEPTH, 3, BLK, UB), SCORE),
            pltpu.VMEM((DEPTH, SLOTS, BLK, UB), bf16),
            pltpu.VMEM((SLOTS,) + block, jnp.float32),
            pltpu.VMEM((ni, SLOTS) + block, jnp.float32),
            pltpu.VMEM((CON_DEPTH, SLOTS) + block, bf16),
            pltpu.VMEM((2 * CHIPS, 128), jnp.int32),
            pltpu.VMEM((2 * CHIPS, 128), jnp.int32),
            pltpu.VMEM((2 * CHIPS, 128), jnp.int32),
            pltpu.SMEM((2 * CHIPS, 128), jnp.int32),
            dma((3,)), dma((2,)),
            dma((ni, PARTS)), dma((ni, PARTS)), dma((no,)), dma((no,)), dma((CHIPS,)), dma((CHIPS,)),
            dma((ni, PARTS)), dma((ni, PARTS)), dma((no,)), dma((no,)),
            dma((DEPTH, 3)), dma((DEPTH, 3)), dma((DEPTH, 3)), dma((DEPTH, 3)),
            dma((CON_DEPTH,)), dma((CHIPS,)), dma((CON_DEPTH,)), dma((PARTS,)), dma((4,)),
        ],
        compiler_params=pltpu.CompilerParams(
            collective_id=0, has_side_effects=True, vmem_limit_bytes=60 * 1024 * 1024),
        name="tree",
    )(req, home, labs, utter, intents)


SCORE = jnp.bfloat16
CHUNK = 16


def gather_kernel(tabs_ref, con_ref, out_ref, con, acc, res, sem_in, sem_out):
    count = con.shape[0]
    core = lax.axis_index("cls") % 2

    def load(i):
        piece = pl.ds(i * CHUNK, CHUNK)
        return pltpu.make_async_copy(con_ref.at[piece], con.at[piece], sem_in.at[i])

    def store(i):
        piece = pl.ds(i * CHUNK, CHUNK)
        return pltpu.make_async_copy(res.at[piece], out_ref.at[piece], sem_out.at[i])

    for i in range(count // CHUNK):
        load(i).start()
    acc[...] = jnp.zeros_like(acc)

    def chunk(i, carry):
        load(i).wait()
        for k in range(CHUNK):
            slot = i * CHUNK + k
            packed = tabs_ref[slot // (2 * CHIPS), slot // 2 % CHIPS, core * 2 + k % 2]

            @pl.when(packed > 0)
            def _():
                b = packed // 8 % BLK_DEV
                acc[b] = acc[b] + con[slot].astype(jnp.float32)
        return carry

    lax.fori_loop(0, count // CHUNK, chunk, 0)
    for i in range(BLK_DEV // CHUNK):
        piece = pl.ds(i * CHUNK, CHUNK)
        res[piece] = acc[piece].astype(res.dtype)
        store(i).start()
    for i in range(BLK_DEV // CHUNK):
        store(i).wait()


def gather(tabs, con):
    count, width = con.shape[0], con.shape[2]
    dma = pltpu.SemaphoreType.DMA
    return pl.pallas_call(
        gather_kernel,
        in_specs=[pl.BlockSpec(memory_space=pltpu.SMEM), pl.BlockSpec(memory_space=pl.ANY)],
        out_specs=pl.BlockSpec(memory_space=pl.ANY),
        scratch_shapes=[
            pltpu.VMEM((count, BLK, width), jnp.bfloat16),
            pltpu.VMEM((BLK_DEV, BLK, width), jnp.float32),
            pltpu.VMEM((BLK_DEV, BLK, width), jnp.bfloat16),
            dma((count // CHUNK,)), dma((BLK_DEV // CHUNK,)),
        ],
        out_shape=jax.ShapeDtypeStruct((BLK_DEV, BLK, width), jnp.bfloat16),
        compiler_params=pltpu.CompilerParams(vmem_limit_bytes=60 * 1024 * 1024),
        name="sum_blocks",
    )(tabs, con)


def shards(utter, intents, req_blocks, req_count, block_home, labels):
    width = intents.shape[1]
    grad_utter, con, tabs = tree(
        req_blocks.reshape(2 * CHIPS, UBD * MOST), block_home.reshape(-1, 128), labels.T,
        utter.reshape(UBD, UB, width), intents.reshape(BLK_DEV, BLK, width))
    grad_intents = gather(tabs, con.reshape(4 * CHIPS, BLK, width))
    return grad_utter.reshape(UBD * UB, width), grad_intents.reshape(BLK_DEV * BLK, width)


def solution(mesh):
    return jax.shard_map(
        shards,
        mesh=mesh,
        in_specs=(
            P(("dp", "cls"), "feat"),
            P(("dp", "cls"), "feat"),
            P(),
            P(),
            P(),
            P(("dp", "cls"), None),
        ),
        out_specs=(P(("dp", "cls"), "feat"), P(("dp", "cls"), "feat")),
        check_vma=False,
    )
```

```python
import jax
import jax.numpy as jnp
from jax import lax
from jax.experimental import pallas as pl
from jax.experimental.pallas import tpu as pltpu
from jax.sharding import PartitionSpec as P

BLK = 128
BLK_DEV = 64
UB = 128
UBD = 8
MOST = 16
GAMMA = 4.0
MARGIN = 0.25

NY, NZ = 4, 8
CHIPS = NY * NZ
SLOTS = 4
DEPTH = 8
CON_DEPTH = 4
LAG_SLOPE = 2
LAG_GRAD = 4
PARTS = 2
PART = UBD // PARTS
ROWS = 32
MESH = pl.DeviceIdType.MESH

NODES = (
    (0, 0, -1, -1, 1),
    (1, 0, 0, 2, 1),
    (0, 1, 0, 0, 1),
    (0, 7, 0, 1, 1),
    (2, 0, 1, 2, 1),
    (3, 1, 2, 3, 0),
    (0, 2, 2, 0, 1),
    (1, 1, 2, 2, 0),
    (1, 7, 3, 2, 0),
    (2, 7, 4, 1, 1),
    (0, 6, 3, 1, 0),
    (3, 2, 6, 3, 0),
    (0, 3, 6, 0, 1),
    (3, 7, 3, 3, 0),
    (2, 6, 9, 1, 1),
    (1, 3, 12, 2, 1),
    (2, 1, 4, 0, 0),
    (0, 4, 12, 0, 1),
    (2, 5, 14, 1, 0),
    (1, 6, 14, 3, 0),
    (3, 6, 14, 2, 0),
    (2, 3, 15, 2, 1),
    (1, 2, 15, 1, 0),
    (3, 4, 17, 3, 0),
    (2, 4, 21, 0, 0),
    (0, 5, 17, 0, 1),
    (2, 2, 21, 1, 0),
    (3, 3, 21, 2, 0),
    (1, 5, 25, 2, 0),
    (3, 5, 25, 3, 0),
    (1, 4, 15, 0, 0),
    (3, 0, 4, 2, 0),
)
TASKS = (
    (("A", 0, 0), ("A", 0, 1),),
    (("A", 2, 0), ("A", 1, 0), ("A", 3, 0), ("A", 1, 1),),
    (("A", 2, 1),),
    (("A", 4, 0), ("A", 3, 1),),
    (("A", 4, 1),),
    (("A", 6, 0),),
    (("A", 6, 1),),
    (("A", 9, 0),),
    (),
    (("A", 9, 1),),
    (),
    (("A", 12, 0),),
    (("A", 12, 1),),
    (("A", 15, 0), ("A", 14, 0),),
    (("A", 14, 1),),
    (("A", 15, 1),),
    (("A", 17, 0),),
    (("A", 17, 1),),
    (("A", 21, 0),),
    (),
    (),
    (("A", 21, 1),),
    (("A", 25, 0),),
    (("A", 25, 1),),
    (("R", 3, 0), ("R", 3, 1),),
    (),
    (),
    (),
    (("R", 14, 0), ("R", 14, 1),),
    (),
    (),
    (("R", 9, 0),),
    (("R", 9, 1),),
    (),
    (("R", 21, 0), ("R", 21, 1),),
    (),
)
LAST = (("R", 25, 0), ("R", 25, 1), ("R", 15, 0), ("R", 17, 0), ("R", 15, 1), ("R", 17, 1), ("R", 4, 0), ("R", 4, 1), ("R", 12, 0), ("R", 12, 1), ("R", 6, 0), ("R", 1, 0), ("R", 6, 1), ("R", 1, 1), ("R", 2, 0), ("R", 2, 1), ("R", 0, 0), ("R", 0, 1),)

DIRS = ((0, 1), (0, -1), (1, 0), (-1, 0))
INNER = [k for k in range(CHIPS) if NODES[k][4]]
OUTER = [k for k in range(CHIPS) if not NODES[k][4]]
SPOT = {k: i for i, k in enumerate(INNER)}
SPOT.update({k: i for i, k in enumerate(OUTER)})
KIDS = {k: [c for c in range(CHIPS) if NODES[c][2] == k] for k in range(CHIPS)}


def tree_kernel(
    req_ref, home_ref, lab_ref, utter_ref, intents_ref,
    gu_ref, con_ref, tabs_ref,
    ag, outer, stage, aglab, rsin, rep, w, ucur, usel, labsel, part, recv, gs, gown, gbuf, cst, lists, eight, reqs, homes, tab, rows_ref,
    sem_in, sem_w, ag_send, ag_recv, out_send, out_recv, lab_send, lab_recv, rs_send, rs_recv, rep_send, rep_recv,
    part_send, part_recv, gs_send, gs_recv, con_send, con_recv, con_loc, sem_out, sem_tab,
):
    z = lax.axis_index("dp")
    cl = lax.axis_index("cls")
    x = lax.axis_index("feat")
    y = cl // 2
    core = cl % 2
    sign = 1 - 2 * core

    def toward(way, back=False):
        dy, dz = DIRS[way]
        flip = -sign if back else sign
        return ((z + NZ + flip * dz) % NZ, (y + NY + flip * dy) % NY * 2 + core, x)

    other = (z, y * 2 + (1 - core), x)

    def peer(o):
        return (z, cl, (x + o) % 4)

    def remote(src, dst, send, recv_sem, device):
        return pltpu.make_async_remote_copy(
            src_ref=src, dst_ref=dst, send_sem=send, recv_sem=recv_sem, device_id=device, device_id_type=MESH)

    def ag_copy(k, h):
        piece = pl.ds(h * PART, PART)
        return remote(ag.at[SPOT[NODES[k][2]], piece], ag.at[SPOT[k], piece],
                      ag_send.at[SPOT[k], h], ag_recv.at[SPOT[k], h], toward(NODES[k][3]))

    def out_copy(k):
        return remote(stage.at[SPOT[k]], outer.at[SPOT[k]], out_send.at[SPOT[k]], out_recv.at[SPOT[k]], toward(NODES[k][3]))

    def lab_copy(k):
        return remote(aglab.at[NODES[k][2]], aglab.at[k], lab_send.at[k], lab_recv.at[k], toward(NODES[k][3]))

    def rs_copy(k, h):
        piece = pl.ds(h * PART, PART)
        return remote(ag.at[SPOT[k], piece], rsin.at[SPOT[k], piece],
                      rs_send.at[SPOT[k], h], rs_recv.at[SPOT[k], h], toward(NODES[k][3], True))

    def rep_copy(k):
        return remote(outer.at[SPOT[k]], rep.at[SPOT[k]], rep_send.at[SPOT[k]], rep_recv.at[SPOT[k]], toward(NODES[k][3], True))

    def part_copy(n, o):
        return remote(part.at[n % DEPTH, (x + o) % 4], recv.at[n % DEPTH, o - 1],
                      part_send.at[n % DEPTH, o - 1], part_recv.at[n % DEPTH, o - 1], peer(o))

    def gs_copy(m, o):
        return remote(gs.at[m % DEPTH, x], gs.at[m % DEPTH, x],
                      gs_send.at[m % DEPTH, o - 1], gs_recv.at[m % DEPTH, o - 1], peer(o))

    def gs_wait(m, o):
        place = gs.at[m % DEPTH, (x + 4 - o) % 4]
        remote(place, place, gs_send.at[m % DEPTH, o - 1], gs_recv.at[m % DEPTH, o - 1], peer(o)).wait_recv()

    def con_far(m):
        return remote(cst.at[m % CON_DEPTH, pl.ds(2 * (1 - core), 2)], con_ref.at[core, m],
                      con_send.at[m % CON_DEPTH], con_recv.at[m], other)

    def con_far_wait(m):
        remote(cst.at[m % CON_DEPTH, pl.ds(2 * (1 - core), 2)], con_ref.at[1 - core, m],
               con_send.at[m % CON_DEPTH], con_recv.at[m], other).wait_recv()

    def con_near(m):
        return pltpu.make_async_copy(
            cst.at[m % CON_DEPTH, pl.ds(2 * core, 2)], con_ref.at[core, m], con_loc.at[m % CON_DEPTH])

    def out_dma(h):
        piece = pl.ds(h * PART, PART)
        return pltpu.make_async_copy(ag.at[0, piece], gu_ref.at[piece], sem_out.at[h])

    own_u = pltpu.make_async_copy(utter_ref, ag.at[0], sem_in.at[0])
    own_w = pltpu.make_async_copy(intents_ref, w.at[pl.ds(core * BLK_DEV, BLK_DEV)], sem_in.at[2])
    far_w = remote(intents_ref, w.at[pl.ds(core * BLK_DEV, BLK_DEV)], sem_w.at[0], sem_w.at[1], other)
    far_w_in = remote(intents_ref, w.at[pl.ds((1 - core) * BLK_DEV, BLK_DEV)], sem_w.at[0], sem_w.at[1], other)
    own_u.start()
    own_w.start()

    barrier = pltpu.get_barrier_semaphore()
    for device in [toward(way) for way in range(4)] + [other, peer(1), peer(2), peer(3)]:
        pl.semaphore_signal(barrier, inc=1, device_id=device, device_id_type=MESH)
    pl.semaphore_wait(barrier, 8)
    own_u.wait()
    for k in range(2):
        for i in range(UBD):
            aglab[0, k * UBD + i:k * UBD + i + 1] = lab_ref[k:k + 1, i * UB:(i + 1) * UB]
    far_w.start()

    tab_near = pltpu.make_async_copy(tab.at[pl.ds(0, CHIPS)], tabs_ref.at[core], sem_tab.at[1])
    tab_far = remote(tab.at[pl.ds(0, CHIPS)], tabs_ref.at[core], sem_tab.at[2], sem_tab.at[3], other)
    tab_in = remote(tab.at[pl.ds(0, CHIPS)], tabs_ref.at[1 - core], sem_tab.at[2], sem_tab.at[3], other)

    def pass_on(k, h):
        if k > 0:
            ag_copy(k, h).wait_recv()
            if h == 0:
                lab_copy(k).wait_recv()
        for c in KIDS[k]:
            if NODES[c][4]:
                ag_copy(c, h).start()
                if h == 0:
                    lab_copy(c).start()

    def pick(k):
        d = k % DEPTH
        if NODES[k][4]:
            for j in range(UBD):
                ucur[j] = ag[SPOT[k], j]
            for c in KIDS[k]:
                if not NODES[c][4]:
                    for s in range(SLOTS):
                        stage[SPOT[c], s] = ucur[block_of(CHIPS + c, s)]
                    out_copy(c).start()
                    lab_copy(c).start()
            for s in range(SLOTS):
                usel[d, s] = ucur[block_of(k, s)]
        else:
            out_copy(k).wait_recv()
            lab_copy(k).wait_recv()
            for s in range(SLOTS):
                usel[d, s] = outer[SPOT[k], s]

    def block_of(k, s):
        return rows_ref[k, s] % 8

    def place_of(k, s):
        return rows_ref[k, s] // 8 % 128

    def make_plan():
        lanes = 128
        for q in range(lists.shape[0] // lanes):
            columns = req_ref[:, q * lanes:(q + 1) * lanes]
            lists[q * lanes:(q + 1) * lanes] = jnp.concatenate(
                [columns, jnp.zeros((lanes - MOST, lanes), jnp.int32)], axis=0).T
        for k in range(CHIPS):
            dy, dz = NODES[k][:2]
            row = (z + NZ - sign * dz) % NZ * 2 * NY + (y + NY - sign * dy) % NY * 2 + core
            eight[k * UBD:(k + 1) * UBD] = lists[pl.ds(pl.multiple_of(row * UBD, UBD), UBD)]
        spot = lax.broadcasted_iota(jnp.int32, (CHIPS, lanes), 1) // MOST
        row = jnp.zeros((CHIPS, lanes), jnp.int32)
        for i in range(UBD):
            row = jnp.where(spot == i, pltpu.roll(eight[pl.ds(i, CHIPS, stride=UBD)], i * MOST, 1), row)
        reqs[0:CHIPS] = row
        table = home_ref[...]
        high = (table // 64).astype(jnp.float32).astype(jnp.bfloat16)
        low = (table % 64).astype(jnp.float32).astype(jnp.bfloat16)
        tall = lax.broadcasted_iota(jnp.int32, (lanes, lanes), 0)
        for k in range(CHIPS):
            ids = reqs[k:k + 1]
            pick_hi = (tall[:32] == ids // lanes).astype(jnp.float32).astype(jnp.bfloat16)
            pick_lo = tall == ids % lanes
            contract = (((0,), (0,)), ((), ()))
            a = lax.dot_general(high, pick_hi, contract, preferred_element_type=jnp.float32)
            b = lax.dot_general(low, pick_hi, contract, preferred_element_type=jnp.float32)
            home = jnp.sum(jnp.where(pick_lo, a * 64.0 + b, 0.0), axis=0, keepdims=True)
            homes[k:k + 1] = jnp.where(ids >= 0, home.astype(jnp.int32), -1)
        here = z * NY + y
        codes = []
        for dy, dz in DIRS:
            codes.append((z + NZ + sign * dz) % NZ * NY + (y + NY + sign * dy) % NY)
        for k in range(CHIPS):
            parent, way = NODES[k][2:4]
            if parent >= 0:
                homes[CHIPS + k:CHIPS + k + 1] = homes[parent:parent + 1] + (here - codes[way]) * 2 * BLK_DEV
                reqs[CHIPS + k:CHIPS + k + 1] = reqs[parent:parent + 1]
            else:
                homes[CHIPS + k:CHIPS + k + 1] = jnp.full((1, lanes), -1, jnp.int32)
                reqs[CHIPS + k:CHIPS + k + 1] = jnp.full((1, lanes), -1, jnp.int32)
        ids, home = reqs[...], homes[...]
        lane = lax.broadcasted_iota(jnp.int32, ids.shape, 1)
        at = lane.astype(jnp.float32)
        packed = jnp.zeros(ids.shape, jnp.int32)

        def total(v):
            return jnp.sum(v.astype(jnp.float32), axis=1, keepdims=True).astype(jnp.int32)

        for o in range(2):
            base = here * 2 * BLK_DEV + o * BLK_DEV
            mine = (ids >= 0) & (home >= base) & (home < base + BLK_DEV)
            first = jnp.min(jnp.where(mine, at, 1000.0), axis=1, keepdims=True).astype(jnp.int32)
            last = jnp.max(jnp.where(mine, at, -1.0), axis=1, keepdims=True).astype(jnp.int32)
            for s, (entry, valid) in enumerate(((first, last >= 0), (last, last > first))):
                hot = mine & (lane == entry)
                block = entry // MOST
                place = total(jnp.where(hot, home - here * 2 * BLK_DEV, 0))
                name = total(jnp.where(hot, ids, 0))
                listed = total(jnp.where((ids >= 0) & (lane // MOST == block), 1, 0))
                value = block + 8 * place + 1024 * listed + 32768 * name
                value = jnp.where(valid, value, 0)
                packed = packed + jnp.where(lane == 2 * o + s, value, 0)
        tab[...] = packed
        fill = pltpu.make_async_copy(tab, rows_ref, sem_tab.at[0])
        fill.start()
        tab_near.start()
        tab_far.start()
        fill.wait()

    def scores(n):
        d = n % DEPTH

        @pl.when(n >= DEPTH)
        def _():
            for o in range(1, 4):
                part_copy(n, o).wait_send()

        mine = block_of(n, x)
        rows = lax.broadcasted_iota(jnp.int32, (UBD, UB), 0)
        for k in range(2):
            labs = aglab[n, k * UBD:(k + 1) * UBD]
            labsel[d, k:k + 1] = jnp.sum(jnp.where(rows == mine, labs, 0), axis=0, keepdims=True)
        for s in range(SLOTS):
            part[d, s] = lax.dot_general(
                w[place_of(n, s)], usel[d, s], (((1,), (1,)), ((), ())),
                preferred_element_type=jnp.float32).astype(part.dtype)
        for o in range(1, 4):
            part_copy(n, o).start()

    def slopes(m):
        d = m % DEPTH

        @pl.when(m >= DEPTH)
        def _():
            for o in range(1, 4):
                gs_copy(m, o).wait_send()

        total = part[d, x].astype(jnp.float32)
        for o in range(1, 4):
            part_copy(m, o).wait_recv()
            total = total + recv[d, o - 1].astype(jnp.float32)
        logits = GAMMA * total
        ids = lax.broadcasted_iota(jnp.int32, (BLK, UB), 0) + (rows_ref[m, x] // 32768) * BLK
        hit = (ids == labsel[d, 0:1]) | (ids == labsel[d, 1:2])
        slope = jax.nn.sigmoid(jnp.where(hit, MARGIN - logits, logits + MARGIN))
        listed = jnp.full((1, UB), rows_ref[m, x] // 1024 % 32, jnp.int32).astype(jnp.float32)
        scale = jnp.where(listed > 0, GAMMA / jnp.maximum(listed, 1.0), 0.0)
        slope = jnp.where(hit, -slope, slope) * scale
        gs[d, x] = slope.astype(jnp.bfloat16)
        for o in range(1, 4):
            gs_copy(m, o).start()

    def grads(m):
        d = m % DEPTH
        e = m % CON_DEPTH

        @pl.when(m >= CON_DEPTH)
        def _():
            con_far(m).wait_send()
            con_near(m).wait()

        for o in range(1, 4):
            gs_wait(m, o)
        for s in range(SLOTS):
            slope = gs[d, s]
            cst[e, s] = jnp.dot(slope, usel[d, s], preferred_element_type=jnp.float32).astype(jnp.bfloat16)
            gown[s] = lax.dot_general(
                slope, w[place_of(m, s)], (((0,), (0,)), ((), ())),
                preferred_element_type=jnp.float32)
        con_far(m).start()
        con_near(m).start()

    def keep(k):
        if NODES[k][4]:
            for s in range(SLOTS):
                gbuf[SPOT[k], s] = gown[s]
        else:
            for s in range(SLOTS):
                outer[SPOT[k], s] = gown[s].astype(jnp.bfloat16)
            rep_copy(k).start()

    def fold(k, h):
        inner = [c for c in KIDS[k] if NODES[c][4]]
        outer_kids = [c for c in KIDS[k] if not NODES[c][4]]
        for c in inner:
            rs_copy(c, h).wait_recv()
            ag_copy(c, h).wait_send()
        if h == 0:
            for c in outer_kids:
                rep_copy(c).wait_recv()
        tiles = UB // ROWS

        def tile(i, carry):
            j = h * PART + i // tiles
            rows = pl.ds(pl.multiple_of(i % tiles * ROWS, ROWS), ROWS)
            total = jnp.zeros((ROWS, ag.shape[3]), jnp.float32)
            for s in range(SLOTS):
                total = total + gbuf[SPOT[k], s, rows] * (block_of(k, s) == j).astype(jnp.float32)
            for c in outer_kids:
                for s in range(SLOTS):
                    share = (block_of(CHIPS + c, s) == j).astype(jnp.float32)
                    total = total + rep[SPOT[c], s, rows].astype(jnp.float32) * share
            for c in inner:
                total = total + rsin[SPOT[c], j, rows].astype(jnp.float32)
            ag[SPOT[k], j, rows] = total.astype(jnp.bfloat16)
            return carry

        lax.fori_loop(0, PART * tiles, tile, 0)
        if k == 0:
            out_dma(h).start()
        else:
            rs_copy(k, h).start()

    def do(tasks):
        for kind, k, h in tasks:
            if kind == "A":
                pass_on(k, h)
            else:
                fold(k, h)

    def step(n, carry):
        for k in range(len(TASKS)):
            if k < CHIPS or TASKS[k]:
                @pl.when(n == k)
                def _():
                    if k > 0:
                        do(TASKS[k])
                    if k < CHIPS:
                        pick(k)
                    if k == 0:
                        own_w.wait()
                        far_w_in.wait_recv()

        @pl.when(n < CHIPS)
        def _():
            scores(n)

        @pl.when((n >= LAG_SLOPE) & (n < CHIPS + LAG_SLOPE))
        def _():
            slopes(n - LAG_SLOPE)

        @pl.when(n >= LAG_GRAD)
        def _():
            grads(n - LAG_GRAD)

        for k in range(CHIPS):
            @pl.when(n == k + LAG_GRAD)
            def _():
                keep(k)
        return carry

    do(TASKS[0])
    make_plan()
    lax.fori_loop(0, CHIPS + LAG_GRAD, step, 0)
    do(LAST)

    for k in range(1, CHIPS):
        lab_copy(k).wait_send()
        if NODES[k][4]:
            for h in range(PARTS):
                rs_copy(k, h).wait_send()
        else:
            out_copy(k).wait_send()
            rep_copy(k).wait_send()

    def drain(n, carry):
        con_far_wait(n)
        return carry

    lax.fori_loop(0, CHIPS, drain, 0)
    for n in range(CHIPS - DEPTH, CHIPS):
        for o in range(1, 4):
            part_copy(n, o).wait_send()
            gs_copy(n, o).wait_send()
    for n in range(CHIPS - CON_DEPTH, CHIPS):
        con_far(n).wait_send()
        con_near(n).wait()
    far_w.wait_send()
    tab_near.wait()
    tab_far.wait_send()
    tab_in.wait_recv()
    for h in range(PARTS):
        out_dma(h).wait()


def tree(req, home, labs, utter, intents):
    width = intents.shape[2]
    block = (UB, width)
    dma = pltpu.SemaphoreType.DMA
    anyspace = pl.BlockSpec(memory_space=pl.ANY)
    vmem = pl.BlockSpec(memory_space=pltpu.VMEM)
    ni, no = len(INNER), len(OUTER)
    bf16 = jnp.bfloat16
    return pl.pallas_call(
        tree_kernel,
        out_shape=(
            jax.ShapeDtypeStruct((UBD,) + block, bf16),
            jax.ShapeDtypeStruct((2, CHIPS, 2) + block, bf16),
            jax.ShapeDtypeStruct((2, CHIPS, 128), jnp.int32),
        ),
        in_specs=[vmem] * 3 + [anyspace] * 2,
        out_specs=(anyspace, anyspace, anyspace),
        scratch_shapes=[
            pltpu.VMEM((ni, UBD) + block, bf16),
            pltpu.VMEM((no, SLOTS) + block, bf16),
            pltpu.VMEM((no, SLOTS) + block, bf16),
            pltpu.VMEM((CHIPS, 2 * UBD, UB), jnp.int32),
            pltpu.VMEM((ni, UBD) + block, bf16),
            pltpu.VMEM((no, SLOTS) + block, bf16),
            pltpu.VMEM((2 * BLK_DEV,) + block, bf16),
            pltpu.VMEM((UBD,) + block, bf16),
            pltpu.VMEM((DEPTH, SLOTS) + block, bf16),
            pltpu.VMEM((DEPTH, 8, UB), jnp.int32),
            pltpu.VMEM((DEPTH, SLOTS, BLK, UB), SCORE),
            pltpu.VMEM((DEPTH, 3, BLK, UB), SCORE),
            pltpu.VMEM((DEPTH, SLOTS, BLK, UB), bf16),
            pltpu.VMEM((SLOTS,) + block, jnp.float32),
            pltpu.VMEM((ni, SLOTS) + block, jnp.float32),
            pltpu.VMEM((CON_DEPTH, SLOTS) + block, bf16),
            pltpu.VMEM((2 * CHIPS * UBD, 128), jnp.int32),
            pltpu.VMEM((CHIPS * UBD, 128), jnp.int32),
            pltpu.VMEM((2 * CHIPS, 128), jnp.int32),
            pltpu.VMEM((2 * CHIPS, 128), jnp.int32),
            pltpu.VMEM((2 * CHIPS, 128), jnp.int32),
            pltpu.SMEM((2 * CHIPS, 128), jnp.int32),
            dma((3,)), dma((2,)),
            dma((ni, PARTS)), dma((ni, PARTS)), dma((no,)), dma((no,)), dma((CHIPS,)), dma((CHIPS,)),
            dma((ni, PARTS)), dma((ni, PARTS)), dma((no,)), dma((no,)),
            dma((DEPTH, 3)), dma((DEPTH, 3)), dma((DEPTH, 3)), dma((DEPTH, 3)),
            dma((CON_DEPTH,)), dma((CHIPS,)), dma((CON_DEPTH,)), dma((PARTS,)), dma((4,)),
        ],
        compiler_params=pltpu.CompilerParams(
            collective_id=0, has_side_effects=True, vmem_limit_bytes=60 * 1024 * 1024),
        name="tree",
    )(req, home, labs, utter, intents)


SCORE = jnp.bfloat16
CHUNK = 16


def gather_kernel(tabs_ref, con_ref, gu_ref, out_ref, gu_out, con, acc, res, gu, sem_in, sem_out, sem_gu):
    count = con.shape[0]
    core = lax.axis_index("cls") % 2

    def load(i):
        piece = pl.ds(i * CHUNK, CHUNK)
        return pltpu.make_async_copy(con_ref.at[piece], con.at[piece], sem_in.at[i])

    def store(i):
        piece = pl.ds(i * CHUNK, CHUNK)
        return pltpu.make_async_copy(res.at[piece], out_ref.at[piece], sem_out.at[i])

    for i in range(count // CHUNK):
        load(i).start()
    gu_load = pltpu.make_async_copy(gu_ref, gu, sem_gu.at[0])
    gu_store = pltpu.make_async_copy(gu, gu_out, sem_gu.at[1])
    gu_load.start()
    acc[...] = jnp.zeros_like(acc)

    def chunk(i, carry):
        load(i).wait()
        half, row = i // (2 * CHIPS // CHUNK), i % (2 * CHIPS // CHUNK) * (CHUNK // 2)
        for k in range(CHUNK):
            b = tabs_ref[half, row + k // 2, core * 2 + k % 2] // 8 % BLK_DEV
            acc[b] = acc[b] + con[i * CHUNK + k].astype(jnp.float32)
        return carry

    lax.fori_loop(0, count // CHUNK, chunk, 0)
    gu_load.wait()
    gu_store.start()
    for i in range(BLK_DEV // CHUNK):
        piece = pl.ds(i * CHUNK, CHUNK)
        res[piece] = acc[piece].astype(res.dtype)
        store(i).start()
    for i in range(BLK_DEV // CHUNK):
        store(i).wait()
    gu_store.wait()


def gather(tabs, con, grad_utter):
    count, width = con.shape[0], con.shape[2]
    dma = pltpu.SemaphoreType.DMA
    return pl.pallas_call(
        gather_kernel,
        in_specs=[pl.BlockSpec(memory_space=pltpu.SMEM)] + [pl.BlockSpec(memory_space=pl.ANY)] * 2,
        out_specs=(pl.BlockSpec(memory_space=pl.ANY),) * 2,
        scratch_shapes=[
            pltpu.VMEM((count, BLK, width), jnp.bfloat16),
            pltpu.VMEM((BLK_DEV, BLK, width), jnp.float32),
            pltpu.VMEM((BLK_DEV, BLK, width), jnp.bfloat16),
            pltpu.VMEM(grad_utter.shape, grad_utter.dtype),
            dma((count // CHUNK,)), dma((BLK_DEV // CHUNK,)), dma((2,)),
        ],
        out_shape=(
            jax.ShapeDtypeStruct((BLK_DEV, BLK, width), jnp.bfloat16),
            jax.ShapeDtypeStruct(grad_utter.shape, grad_utter.dtype),
        ),
        compiler_params=pltpu.CompilerParams(vmem_limit_bytes=60 * 1024 * 1024),
        name="sum_blocks",
    )(tabs, con, grad_utter)


def shards(utter, intents, req_blocks, req_count, block_home, labels):
    width = intents.shape[1]
    grad_utter, con, tabs = tree(
        req_blocks.T, block_home.reshape(-1, 128), labels.T,
        utter.reshape(UBD, UB, width), intents.reshape(BLK_DEV, BLK, width))
    grad_intents, grad_utter = gather(tabs, con.reshape(4 * CHIPS, BLK, width), grad_utter)
    return grad_utter.reshape(UBD * UB, width), grad_intents.reshape(BLK_DEV * BLK, width)


def solution(mesh):
    return jax.shard_map(
        shards,
        mesh=mesh,
        in_specs=(
            P(("dp", "cls"), "feat"),
            P(("dp", "cls"), "feat"),
            P(),
            P(),
            P(),
            P(("dp", "cls"), None),
        ),
        out_specs=(P(("dp", "cls"), "feat"), P(("dp", "cls"), "feat")),
        check_vma=False,
    )
```

```python
import jax
import jax.numpy as jnp
from jax import lax
from jax.experimental import pallas as pl
from jax.experimental.pallas import tpu as pltpu
from jax.sharding import PartitionSpec as P

BLK = 128
BLK_DEV = 64
UB = 128
UBD = 8
MOST = 16
GAMMA = 4.0
MARGIN = 0.25

NY, NZ = 4, 8
CHIPS = NY * NZ
SLOTS = 4
DEPTH = 8
CON_DEPTH = 4
LAG_SLOPE = 2
LAG_GRAD = 4
PARTS = 2
PART = UBD // PARTS
ROWS = 32
MESH = pl.DeviceIdType.MESH

NODES = (
    (0, 0, -1, -1, 1),
    (1, 0, 0, 2, 1),
    (0, 1, 0, 0, 1),
    (0, 7, 0, 1, 1),
    (2, 0, 1, 2, 1),
    (3, 1, 2, 3, 0),
    (0, 2, 2, 0, 1),
    (1, 1, 2, 2, 0),
    (1, 7, 3, 2, 0),
    (2, 7, 4, 1, 1),
    (0, 6, 3, 1, 0),
    (3, 2, 6, 3, 0),
    (0, 3, 6, 0, 1),
    (3, 7, 3, 3, 0),
    (2, 6, 9, 1, 1),
    (1, 3, 12, 2, 1),
    (2, 1, 4, 0, 0),
    (0, 4, 12, 0, 1),
    (2, 5, 14, 1, 0),
    (1, 6, 14, 3, 0),
    (3, 6, 14, 2, 0),
    (2, 3, 15, 2, 1),
    (1, 2, 15, 1, 0),
    (3, 4, 17, 3, 0),
    (2, 4, 21, 0, 0),
    (0, 5, 17, 0, 1),
    (2, 2, 21, 1, 0),
    (3, 3, 21, 2, 0),
    (1, 5, 25, 2, 0),
    (3, 5, 25, 3, 0),
    (1, 4, 15, 0, 0),
    (3, 0, 4, 2, 0),
)
TASKS = (
    (("A", 0, 0), ("A", 0, 1),),
    (("A", 2, 0), ("A", 1, 0), ("A", 3, 0), ("A", 1, 1),),
    (("A", 2, 1),),
    (("A", 4, 0), ("A", 3, 1),),
    (("A", 4, 1),),
    (("A", 6, 0),),
    (("A", 6, 1),),
    (("A", 9, 0),),
    (),
    (("A", 9, 1),),
    (),
    (("A", 12, 0),),
    (("A", 12, 1),),
    (("A", 15, 0), ("A", 14, 0),),
    (("A", 14, 1),),
    (("A", 15, 1),),
    (("A", 17, 0),),
    (("A", 17, 1),),
    (("A", 21, 0),),
    (),
    (),
    (("A", 21, 1),),
    (("A", 25, 0),),
    (("A", 25, 1),),
    (("R", 3, 0), ("R", 3, 1),),
    (),
    (),
    (),
    (("R", 14, 0), ("R", 14, 1),),
    (),
    (),
    (("R", 9, 0),),
    (("R", 9, 1),),
    (),
    (("R", 21, 0), ("R", 21, 1),),
    (),
)
LAST = (("R", 25, 0), ("R", 25, 1), ("R", 15, 0), ("R", 17, 0), ("R", 15, 1), ("R", 17, 1), ("R", 4, 0), ("R", 4, 1), ("R", 12, 0), ("R", 12, 1), ("R", 6, 0), ("R", 1, 0), ("R", 6, 1), ("R", 1, 1), ("R", 2, 0), ("R", 2, 1), ("R", 0, 0), ("R", 0, 1),)
EARLY = ()

DIRS = ((0, 1), (0, -1), (1, 0), (-1, 0))
INNER = [k for k in range(CHIPS) if NODES[k][4]]
OUTER = [k for k in range(CHIPS) if not NODES[k][4]]
SPOT = {k: i for i, k in enumerate(INNER)}
SPOT.update({k: i for i, k in enumerate(OUTER)})
KIDS = {k: [c for c in range(CHIPS) if NODES[c][2] == k] for k in range(CHIPS)}


def tree_kernel(
    req_ref, home_ref, lab_ref, utter_ref, intents_ref,
    gu_ref, con_ref, tabs_ref,
    ag, outer, stage, aglab, rsin, rep, w, ucur, usel, labsel, part, recv, gs, gown, gbuf, cst, lists, eight, reqs, homes, tab, rows_ref,
    sem_in, sem_w, ag_send, ag_recv, out_send, out_recv, lab_send, lab_recv, rs_send, rs_recv, rep_send, rep_recv,
    part_send, part_recv, gs_send, gs_recv, con_send, con_recv, con_loc, sem_out, sem_tab,
):
    z = lax.axis_index("dp")
    cl = lax.axis_index("cls")
    x = lax.axis_index("feat")
    y = cl // 2
    core = cl % 2
    sign = 1 - 2 * core

    def toward(way, back=False):
        dy, dz = DIRS[way]
        flip = -sign if back else sign
        return ((z + NZ + flip * dz) % NZ, (y + NY + flip * dy) % NY * 2 + core, x)

    other = (z, y * 2 + (1 - core), x)

    def peer(o):
        return (z, cl, (x + o) % 4)

    def remote(src, dst, send, recv_sem, device):
        return pltpu.make_async_remote_copy(
            src_ref=src, dst_ref=dst, send_sem=send, recv_sem=recv_sem, device_id=device, device_id_type=MESH)

    def ag_copy(k, h):
        piece = pl.ds(h * PART, PART)
        return remote(ag.at[SPOT[NODES[k][2]], piece], ag.at[SPOT[k], piece],
                      ag_send.at[SPOT[k], h], ag_recv.at[SPOT[k], h], toward(NODES[k][3]))

    def out_copy(k):
        return remote(stage.at[SPOT[k]], outer.at[SPOT[k]], out_send.at[SPOT[k]], out_recv.at[SPOT[k]], toward(NODES[k][3]))

    def lab_copy(k):
        return remote(aglab.at[NODES[k][2]], aglab.at[k], lab_send.at[k], lab_recv.at[k], toward(NODES[k][3]))

    def rs_copy(k, h):
        piece = pl.ds(h * PART, PART)
        return remote(ag.at[SPOT[k], piece], rsin.at[SPOT[k], piece],
                      rs_send.at[SPOT[k], h], rs_recv.at[SPOT[k], h], toward(NODES[k][3], True))

    def rep_copy(k):
        return remote(outer.at[SPOT[k]], rep.at[SPOT[k]], rep_send.at[SPOT[k]], rep_recv.at[SPOT[k]], toward(NODES[k][3], True))

    def part_copy(n, o):
        return remote(part.at[n % DEPTH, (x + o) % 4], recv.at[n % DEPTH, o - 1],
                      part_send.at[n % DEPTH, o - 1], part_recv.at[n % DEPTH, o - 1], peer(o))

    def gs_copy(m, o):
        return remote(gs.at[m % DEPTH, x], gs.at[m % DEPTH, x],
                      gs_send.at[m % DEPTH, o - 1], gs_recv.at[m % DEPTH, o - 1], peer(o))

    def gs_wait(m, o):
        place = gs.at[m % DEPTH, (x + 4 - o) % 4]
        remote(place, place, gs_send.at[m % DEPTH, o - 1], gs_recv.at[m % DEPTH, o - 1], peer(o)).wait_recv()

    def con_far(m):
        return remote(cst.at[m % CON_DEPTH, pl.ds(2 * (1 - core), 2)], con_ref.at[core, m],
                      con_send.at[m % CON_DEPTH], con_recv.at[m], other)

    def con_far_wait(m):
        remote(cst.at[m % CON_DEPTH, pl.ds(2 * (1 - core), 2)], con_ref.at[1 - core, m],
               con_send.at[m % CON_DEPTH], con_recv.at[m], other).wait_recv()

    def con_near(m):
        return pltpu.make_async_copy(
            cst.at[m % CON_DEPTH, pl.ds(2 * core, 2)], con_ref.at[core, m], con_loc.at[m % CON_DEPTH])

    def out_dma(h):
        piece = pl.ds(h * PART, PART)
        return pltpu.make_async_copy(ag.at[0, piece], gu_ref.at[piece], sem_out.at[h])

    own_u = pltpu.make_async_copy(utter_ref, ag.at[0], sem_in.at[0])
    own_w = pltpu.make_async_copy(intents_ref, w.at[pl.ds(core * BLK_DEV, BLK_DEV)], sem_in.at[2])
    far_w = remote(intents_ref, w.at[pl.ds(core * BLK_DEV, BLK_DEV)], sem_w.at[0], sem_w.at[1], other)
    far_w_in = remote(intents_ref, w.at[pl.ds((1 - core) * BLK_DEV, BLK_DEV)], sem_w.at[0], sem_w.at[1], other)
    own_u.start()
    own_w.start()

    barrier = pltpu.get_barrier_semaphore()
    for device in [toward(way) for way in range(4)] + [other, peer(1), peer(2), peer(3)]:
        pl.semaphore_signal(barrier, inc=1, device_id=device, device_id_type=MESH)
    pl.semaphore_wait(barrier, 8)
    own_u.wait()
    for k in range(2):
        for i in range(UBD):
            aglab[0, k * UBD + i:k * UBD + i + 1] = lab_ref[k:k + 1, i * UB:(i + 1) * UB]
    far_w.start()

    tab_near = pltpu.make_async_copy(tab.at[pl.ds(0, CHIPS)], tabs_ref.at[core], sem_tab.at[1])
    tab_far = remote(tab.at[pl.ds(0, CHIPS)], tabs_ref.at[core], sem_tab.at[2], sem_tab.at[3], other)
    tab_in = remote(tab.at[pl.ds(0, CHIPS)], tabs_ref.at[1 - core], sem_tab.at[2], sem_tab.at[3], other)

    def pass_on(k, h):
        if k > 0:
            ag_copy(k, h).wait_recv()
            if h == 0:
                lab_copy(k).wait_recv()
        for c in KIDS[k]:
            if NODES[c][4]:
                ag_copy(c, h).start()
                if h == 0:
                    lab_copy(c).start()

    def pick(k):
        d = k % DEPTH
        if NODES[k][4]:
            for j in range(UBD):
                ucur[j] = ag[SPOT[k], j]
            for c in KIDS[k]:
                if not NODES[c][4]:
                    for s in range(SLOTS):
                        stage[SPOT[c], s] = ucur[block_of(CHIPS + c, s)]
                    out_copy(c).start()
                    lab_copy(c).start()
            for s in range(SLOTS):
                usel[d, s] = ucur[block_of(k, s)]
        else:
            out_copy(k).wait_recv()
            lab_copy(k).wait_recv()
            for s in range(SLOTS):
                usel[d, s] = outer[SPOT[k], s]

    def block_of(k, s):
        return rows_ref[k, s] % 8

    def place_of(k, s):
        return rows_ref[k, s] // 8 % 128

    def make_plan():
        lanes = 128
        for q in range(lists.shape[0] // lanes):
            columns = req_ref[:, q * lanes:(q + 1) * lanes]
            lists[q * lanes:(q + 1) * lanes] = jnp.concatenate(
                [columns, jnp.zeros((lanes - MOST, lanes), jnp.int32)], axis=0).T
        for k in range(CHIPS):
            dy, dz = NODES[k][:2]
            row = (z + NZ - sign * dz) % NZ * 2 * NY + (y + NY - sign * dy) % NY * 2 + core
            eight[k * UBD:(k + 1) * UBD] = lists[pl.ds(pl.multiple_of(row * UBD, UBD), UBD)]
        spot = lax.broadcasted_iota(jnp.int32, (CHIPS, lanes), 1) // MOST
        row = jnp.zeros((CHIPS, lanes), jnp.int32)
        for i in range(UBD):
            row = jnp.where(spot == i, pltpu.roll(eight[pl.ds(i, CHIPS, stride=UBD)], i * MOST, 1), row)
        reqs[0:CHIPS] = row
        table = home_ref[...]
        high = (table // 64).astype(jnp.float32).astype(jnp.bfloat16)
        low = (table % 64).astype(jnp.float32).astype(jnp.bfloat16)
        tall = lax.broadcasted_iota(jnp.int32, (lanes, lanes), 0)
        for k in range(CHIPS):
            ids = reqs[k:k + 1]
            pick_hi = (tall[:32] == ids // lanes).astype(jnp.float32).astype(jnp.bfloat16)
            pick_lo = tall == ids % lanes
            contract = (((0,), (0,)), ((), ()))
            a = lax.dot_general(high, pick_hi, contract, preferred_element_type=jnp.float32)
            b = lax.dot_general(low, pick_hi, contract, preferred_element_type=jnp.float32)
            home = jnp.sum(jnp.where(pick_lo, a * 64.0 + b, 0.0), axis=0, keepdims=True)
            homes[k:k + 1] = jnp.where(ids >= 0, home.astype(jnp.int32), -1)
        here = z * NY + y
        codes = []
        for dy, dz in DIRS:
            codes.append((z + NZ + sign * dz) % NZ * NY + (y + NY + sign * dy) % NY)
        for k in range(CHIPS):
            parent, way = NODES[k][2:4]
            if parent >= 0:
                homes[CHIPS + k:CHIPS + k + 1] = homes[parent:parent + 1] + (here - codes[way]) * 2 * BLK_DEV
                reqs[CHIPS + k:CHIPS + k + 1] = reqs[parent:parent + 1]
            else:
                homes[CHIPS + k:CHIPS + k + 1] = jnp.full((1, lanes), -1, jnp.int32)
                reqs[CHIPS + k:CHIPS + k + 1] = jnp.full((1, lanes), -1, jnp.int32)
        ids, home = reqs[...], homes[...]
        lane = lax.broadcasted_iota(jnp.int32, ids.shape, 1)
        at = lane.astype(jnp.float32)
        packed = jnp.zeros(ids.shape, jnp.int32)

        def total(v):
            return jnp.sum(v.astype(jnp.float32), axis=1, keepdims=True).astype(jnp.int32)

        for o in range(2):
            base = here * 2 * BLK_DEV + o * BLK_DEV
            mine = (ids >= 0) & (home >= base) & (home < base + BLK_DEV)
            first = jnp.min(jnp.where(mine, at, 1000.0), axis=1, keepdims=True).astype(jnp.int32)
            last = jnp.max(jnp.where(mine, at, -1.0), axis=1, keepdims=True).astype(jnp.int32)
            for s, (entry, valid) in enumerate(((first, last >= 0), (last, last > first))):
                hot = mine & (lane == entry)
                block = entry // MOST
                place = total(jnp.where(hot, home - here * 2 * BLK_DEV, 0))
                name = total(jnp.where(hot, ids, 0))
                listed = total(jnp.where((ids >= 0) & (lane // MOST == block), 1, 0))
                value = block + 8 * place + 1024 * listed + 32768 * name
                value = jnp.where(valid, value, 0)
                packed = packed + jnp.where(lane == 2 * o + s, value, 0)
        tab[...] = packed
        fill = pltpu.make_async_copy(tab, rows_ref, sem_tab.at[0])
        fill.start()
        tab_near.start()
        tab_far.start()
        fill.wait()

    def scores(n):
        d = n % DEPTH

        @pl.when(n >= DEPTH)
        def _():
            for o in range(1, 4):
                part_copy(n, o).wait_send()

        mine = block_of(n, x)
        rows = lax.broadcasted_iota(jnp.int32, (UBD, UB), 0)
        for k in range(2):
            labs = aglab[n, k * UBD:(k + 1) * UBD]
            labsel[d, k:k + 1] = jnp.sum(jnp.where(rows == mine, labs, 0), axis=0, keepdims=True)
        for s in range(SLOTS):
            part[d, s] = lax.dot_general(
                w[place_of(n, s)], usel[d, s], (((1,), (1,)), ((), ())),
                preferred_element_type=jnp.float32).astype(part.dtype)
        for o in range(1, 4):
            part_copy(n, o).start()

    def slopes(m):
        d = m % DEPTH

        @pl.when(m >= DEPTH)
        def _():
            for o in range(1, 4):
                gs_copy(m, o).wait_send()

        total = part[d, x].astype(jnp.float32)
        for o in range(1, 4):
            part_copy(m, o).wait_recv()
            total = total + recv[d, o - 1].astype(jnp.float32)
        logits = GAMMA * total
        ids = lax.broadcasted_iota(jnp.int32, (BLK, UB), 0) + (rows_ref[m, x] // 32768) * BLK
        hit = (ids == labsel[d, 0:1]) | (ids == labsel[d, 1:2])
        slope = jax.nn.sigmoid(jnp.where(hit, MARGIN - logits, logits + MARGIN))
        listed = jnp.full((1, UB), rows_ref[m, x] // 1024 % 32, jnp.int32).astype(jnp.float32)
        scale = jnp.where(listed > 0, GAMMA / jnp.maximum(listed, 1.0), 0.0)
        slope = jnp.where(hit, -slope, slope) * scale
        gs[d, x] = slope.astype(jnp.bfloat16)
        for o in range(1, 4):
            gs_copy(m, o).start()

    def grads(m):
        d = m % DEPTH
        e = m % CON_DEPTH

        @pl.when(m >= CON_DEPTH)
        def _():
            con_far(m).wait_send()
            con_near(m).wait()

        for o in range(1, 4):
            gs_wait(m, o)
        for s in range(SLOTS):
            slope = gs[d, s]
            cst[e, s] = jnp.dot(slope, usel[d, s], preferred_element_type=jnp.float32).astype(jnp.bfloat16)
            gown[s] = lax.dot_general(
                slope, w[place_of(m, s)], (((0,), (0,)), ((), ())),
                preferred_element_type=jnp.float32)
        con_far(m).start()
        con_near(m).start()

    def keep(k):
        if NODES[k][4]:
            for s in range(SLOTS):
                gbuf[SPOT[k], s] = gown[s]
        else:
            for s in range(SLOTS):
                outer[SPOT[k], s] = gown[s].astype(jnp.bfloat16)
            rep_copy(k).start()

    def fold(k, h):
        inner = [c for c in KIDS[k] if NODES[c][4]]
        outer_kids = [c for c in KIDS[k] if not NODES[c][4]]
        for c in inner:
            rs_copy(c, h).wait_recv()
            ag_copy(c, h).wait_send()
        if h == 0:
            for c in outer_kids:
                rep_copy(c).wait_recv()
        tiles = UB // ROWS

        def tile(i, carry):
            j = h * PART + i // tiles
            rows = pl.ds(pl.multiple_of(i % tiles * ROWS, ROWS), ROWS)
            total = jnp.zeros((ROWS, ag.shape[3]), jnp.float32)
            for s in range(SLOTS):
                total = total + gbuf[SPOT[k], s, rows] * (block_of(k, s) == j).astype(jnp.float32)
            for c in outer_kids:
                for s in range(SLOTS):
                    share = (block_of(CHIPS + c, s) == j).astype(jnp.float32)
                    total = total + rep[SPOT[c], s, rows].astype(jnp.float32) * share
            for c in inner:
                total = total + rsin[SPOT[c], j, rows].astype(jnp.float32)
            ag[SPOT[k], j, rows] = total.astype(jnp.bfloat16)
            return carry

        lax.fori_loop(0, PART * tiles, tile, 0)
        if k == 0:
            out_dma(h).start()
        else:
            rs_copy(k, h).start()

    def do(tasks):
        for kind, k, h in tasks:
            if kind == "A":
                pass_on(k, h)
            else:
                fold(k, h)

    def step(n, carry):
        for k in range(len(TASKS)):
            if k < CHIPS or TASKS[k]:
                @pl.when(n == k)
                def _():
                    if k > 0:
                        do(TASKS[k])
                    if k < CHIPS:
                        pick(k)
                    if k == 0:
                        do(EARLY)
                        own_w.wait()
                        far_w_in.wait_recv()

        @pl.when(n < CHIPS)
        def _():
            scores(n)

        @pl.when((n >= LAG_SLOPE) & (n < CHIPS + LAG_SLOPE))
        def _():
            slopes(n - LAG_SLOPE)

        @pl.when(n >= LAG_GRAD)
        def _():
            grads(n - LAG_GRAD)

        for k in range(CHIPS):
            @pl.when(n == k + LAG_GRAD)
            def _():
                keep(k)
        return carry

    do(TASKS[0])
    make_plan()
    lax.fori_loop(0, CHIPS + LAG_GRAD, step, 0)
    do(LAST[:-2 * PARTS])

    for k in range(1, CHIPS):
        lab_copy(k).wait_send()
        if not NODES[k][4]:
            out_copy(k).wait_send()
            rep_copy(k).wait_send()

    def drain(n, carry):
        con_far_wait(n)
        return carry

    lax.fori_loop(0, CHIPS, drain, 0)
    for n in range(CHIPS - DEPTH, CHIPS):
        for o in range(1, 4):
            part_copy(n, o).wait_send()
            gs_copy(n, o).wait_send()
    for n in range(CHIPS - CON_DEPTH, CHIPS):
        con_far(n).wait_send()
        con_near(n).wait()
    far_w.wait_send()
    tab_near.wait()
    tab_far.wait_send()
    tab_in.wait_recv()
    do(LAST[-2 * PARTS:])
    for k in INNER[1:]:
        for h in range(PARTS):
            rs_copy(k, h).wait_send()
    for h in range(PARTS):
        out_dma(h).wait()


def tree(req, home, labs, utter, intents):
    width = intents.shape[2]
    block = (UB, width)
    dma = pltpu.SemaphoreType.DMA
    anyspace = pl.BlockSpec(memory_space=pl.ANY)
    vmem = pl.BlockSpec(memory_space=pltpu.VMEM)
    ni, no = len(INNER), len(OUTER)
    bf16 = jnp.bfloat16
    return pl.pallas_call(
        tree_kernel,
        out_shape=(
            jax.ShapeDtypeStruct((UBD,) + block, bf16),
            jax.ShapeDtypeStruct((2, CHIPS, 2) + block, bf16),
            jax.ShapeDtypeStruct((2, CHIPS, 128), jnp.int32),
        ),
        in_specs=[vmem] * 3 + [anyspace] * 2,
        out_specs=(anyspace, anyspace, anyspace),
        scratch_shapes=[
            pltpu.VMEM((ni, UBD) + block, bf16),
            pltpu.VMEM((no, SLOTS) + block, bf16),
            pltpu.VMEM((no, SLOTS) + block, bf16),
            pltpu.VMEM((CHIPS, 2 * UBD, UB), jnp.int32),
            pltpu.VMEM((ni, UBD) + block, bf16),
            pltpu.VMEM((no, SLOTS) + block, bf16),
            pltpu.VMEM((2 * BLK_DEV,) + block, bf16),
            pltpu.VMEM((UBD,) + block, bf16),
            pltpu.VMEM((DEPTH, SLOTS) + block, bf16),
            pltpu.VMEM((DEPTH, 8, UB), jnp.int32),
            pltpu.VMEM((DEPTH, SLOTS, BLK, UB), SCORE),
            pltpu.VMEM((DEPTH, 3, BLK, UB), SCORE),
            pltpu.VMEM((DEPTH, SLOTS, BLK, UB), bf16),
            pltpu.VMEM((SLOTS,) + block, jnp.float32),
            pltpu.VMEM((ni, SLOTS) + block, jnp.float32),
            pltpu.VMEM((CON_DEPTH, SLOTS) + block, bf16),
            pltpu.VMEM((2 * CHIPS * UBD, 128), jnp.int32),
            pltpu.VMEM((CHIPS * UBD, 128), jnp.int32),
            pltpu.VMEM((2 * CHIPS, 128), jnp.int32),
            pltpu.VMEM((2 * CHIPS, 128), jnp.int32),
            pltpu.VMEM((2 * CHIPS, 128), jnp.int32),
            pltpu.SMEM((2 * CHIPS, 128), jnp.int32),
            dma((3,)), dma((2,)),
            dma((ni, PARTS)), dma((ni, PARTS)), dma((no,)), dma((no,)), dma((CHIPS,)), dma((CHIPS,)),
            dma((ni, PARTS)), dma((ni, PARTS)), dma((no,)), dma((no,)),
            dma((DEPTH, 3)), dma((DEPTH, 3)), dma((DEPTH, 3)), dma((DEPTH, 3)),
            dma((CON_DEPTH,)), dma((CHIPS,)), dma((CON_DEPTH,)), dma((PARTS,)), dma((4,)),
        ],
        compiler_params=pltpu.CompilerParams(
            collective_id=0, has_side_effects=True, vmem_limit_bytes=60 * 1024 * 1024),
        name="tree",
    )(req, home, labs, utter, intents)


SCORE = jnp.bfloat16
CHUNK = 16
OUT = 8


def gather_kernel(tabs_hbm, con_ref, gu_ref, out_ref, gu_out, tabs_ref, con, acc, res, gu, sem_in, sem_out, sem_gu):
    count = con.shape[0]
    core = lax.axis_index("cls") % 2

    def load(i):
        piece = pl.ds(i * CHUNK, CHUNK)
        return pltpu.make_async_copy(con_ref.at[piece], con.at[piece], sem_in.at[i])

    def store(i):
        piece = pl.ds(i * OUT, OUT)
        return pltpu.make_async_copy(res.at[piece], out_ref.at[piece], sem_out.at[i])

    for i in range(count // CHUNK):
        load(i).start()
    gu_load = pltpu.make_async_copy(gu_ref, gu, sem_gu.at[0])
    gu_store = pltpu.make_async_copy(gu, gu_out, sem_gu.at[1])
    gu_load.start()
    tabs_load = pltpu.make_async_copy(tabs_hbm, tabs_ref, sem_gu.at[2])
    tabs_load.start()
    acc[...] = jnp.zeros_like(acc)
    tabs_load.wait()

    def chunk(i, carry):
        load(i).wait()
        half, row = i // (2 * CHIPS // CHUNK), i % (2 * CHIPS // CHUNK) * (CHUNK // 2)
        for k in range(CHUNK):
            b = tabs_ref[half, row + k // 2, core * 2 + k % 2] // 8 % BLK_DEV
            acc[b] = acc[b] + con[i * CHUNK + k].astype(jnp.float32)
        return carry

    lax.fori_loop(0, count // CHUNK, chunk, 0)
    gu_load.wait()
    gu_store.start()
    for i in range(BLK_DEV // OUT):
        piece = pl.ds(i * OUT, OUT)
        res[piece] = acc[piece].astype(res.dtype)
        store(i).start()
    for i in range(BLK_DEV // OUT):
        store(i).wait()
    gu_store.wait()


def gather(tabs, con, grad_utter):
    count, width = con.shape[0], con.shape[2]
    dma = pltpu.SemaphoreType.DMA
    return pl.pallas_call(
        gather_kernel,
        in_specs=[pl.BlockSpec(memory_space=pl.ANY)] * 3,
        out_specs=(pl.BlockSpec(memory_space=pl.ANY),) * 2,
        scratch_shapes=[
            pltpu.SMEM(tabs.shape, jnp.int32),
            pltpu.VMEM((count, BLK, width), jnp.bfloat16),
            pltpu.VMEM((BLK_DEV, BLK, width), jnp.float32),
            pltpu.VMEM((BLK_DEV, BLK, width), jnp.bfloat16),
            pltpu.VMEM(grad_utter.shape, grad_utter.dtype),
            dma((count // CHUNK,)), dma((BLK_DEV // OUT,)), dma((3,)),
        ],
        out_shape=(
            jax.ShapeDtypeStruct((BLK_DEV, BLK, width), jnp.bfloat16),
            jax.ShapeDtypeStruct(grad_utter.shape, grad_utter.dtype),
        ),
        compiler_params=pltpu.CompilerParams(vmem_limit_bytes=60 * 1024 * 1024),
        name="sum_blocks",
    )(tabs, con, grad_utter)


def shards(utter, intents, req_blocks, req_count, block_home, labels):
    width = intents.shape[1]
    grad_utter, con, tabs = tree(
        req_blocks.T, block_home.reshape(-1, 128), labels.T,
        utter.reshape(UBD, UB, width), intents.reshape(BLK_DEV, BLK, width))
    grad_intents, grad_utter = gather(tabs, con.reshape(4 * CHIPS, BLK, width), grad_utter)
    return grad_utter.reshape(UBD * UB, width), grad_intents.reshape(BLK_DEV * BLK, width)


def solution(mesh):
    return jax.shard_map(
        shards,
        mesh=mesh,
        in_specs=(
            P(("dp", "cls"), "feat"),
            P(("dp", "cls"), "feat"),
            P(),
            P(),
            P(),
            P(("dp", "cls"), None),
        ),
        out_specs=(P(("dp", "cls"), "feat"), P(("dp", "cls"), "feat")),
        check_vma=False,
    )
```

```python
import jax
import jax.numpy as jnp
from jax import lax
from jax.experimental import pallas as pl
from jax.experimental.pallas import tpu as pltpu
from jax.sharding import PartitionSpec as P

BLK = 128
BLK_DEV = 64
UB = 128
UBD = 8
MOST = 16
GAMMA = 4.0
MARGIN = 0.25

NY, NZ = 4, 8
CHIPS = NY * NZ
SLOTS = 4
DEPTH = 8
CON_DEPTH = 4
LAG_SLOPE = 2
LAG_GRAD = 4
PARTS = 2
PART = UBD // PARTS
ROWS = 32
MESH = pl.DeviceIdType.MESH

NODES = (
    (0, 0, -1, -1, 1),
    (1, 0, 0, 2, 1),
    (0, 1, 0, 0, 1),
    (0, 7, 0, 1, 1),
    (2, 0, 1, 2, 1),
    (3, 1, 2, 3, 0),
    (0, 2, 2, 0, 1),
    (1, 1, 2, 2, 0),
    (1, 7, 3, 2, 0),
    (2, 7, 4, 1, 1),
    (0, 6, 3, 1, 0),
    (3, 2, 6, 3, 0),
    (0, 3, 6, 0, 1),
    (3, 7, 3, 3, 0),
    (2, 6, 9, 1, 1),
    (1, 3, 12, 2, 1),
    (2, 1, 4, 0, 0),
    (0, 4, 12, 0, 1),
    (2, 5, 14, 1, 0),
    (1, 6, 14, 3, 0),
    (3, 6, 14, 2, 0),
    (2, 3, 15, 2, 1),
    (1, 2, 15, 1, 0),
    (3, 4, 17, 3, 0),
    (2, 4, 21, 0, 0),
    (0, 5, 17, 0, 1),
    (2, 2, 21, 1, 0),
    (3, 3, 21, 2, 0),
    (1, 5, 25, 2, 0),
    (3, 5, 25, 3, 0),
    (1, 4, 15, 0, 0),
    (3, 0, 4, 2, 0),
)
TASKS = (
    (("A", 0, 0), ("A", 0, 1),),
    (("A", 2, 0), ("A", 1, 0), ("A", 3, 0), ("A", 1, 1),),
    (("A", 2, 1),),
    (("A", 4, 0), ("A", 3, 1),),
    (("A", 4, 1),),
    (("A", 6, 0),),
    (("A", 6, 1),),
    (("A", 9, 0),),
    (),
    (("A", 9, 1),),
    (),
    (("A", 12, 0),),
    (("A", 12, 1),),
    (("A", 15, 0), ("A", 14, 0),),
    (("A", 14, 1),),
    (("A", 15, 1),),
    (("A", 17, 0),),
    (("A", 17, 1),),
    (("A", 21, 0),),
    (),
    (),
    (("A", 21, 1),),
    (("A", 25, 0),),
    (("A", 25, 1),),
    (("R", 3, 0), ("R", 3, 1),),
    (),
    (),
    (),
    (("R", 14, 0), ("R", 14, 1),),
    (),
    (),
    (("R", 9, 0),),
    (("R", 9, 1),),
    (),
    (("R", 21, 0), ("R", 21, 1),),
    (),
)
LAST = (("R", 25, 0), ("R", 25, 1), ("R", 15, 0), ("R", 17, 0), ("R", 15, 1), ("R", 17, 1), ("R", 4, 0), ("R", 4, 1), ("R", 12, 0), ("R", 12, 1), ("R", 6, 0), ("R", 1, 0), ("R", 6, 1), ("R", 1, 1), ("R", 2, 0), ("R", 2, 1), ("R", 0, 0), ("R", 0, 1),)
EARLY = ()

DIRS = ((0, 1), (0, -1), (1, 0), (-1, 0))
INNER = [k for k in range(CHIPS) if NODES[k][4]]
OUTER = [k for k in range(CHIPS) if not NODES[k][4]]
SPOT = {k: i for i, k in enumerate(INNER)}
SPOT.update({k: i for i, k in enumerate(OUTER)})
KIDS = {k: [c for c in range(CHIPS) if NODES[c][2] == k] for k in range(CHIPS)}


def tree_kernel(
    req_ref, home_ref, lab_ref, utter_ref, intents_ref,
    gu_ref, con_ref, tabs_ref,
    ag, outer, stage, aglab, rsin, rep, w, ucur, usel, labsel, part, recv, gs, gown, gbuf, cst, lists, eight, reqs, homes, tab, rows_ref,
    sem_in, sem_w, ag_send, ag_recv, out_send, out_recv, lab_send, lab_recv, rs_send, rs_recv, rep_send, rep_recv,
    part_send, part_recv, gs_send, gs_recv, con_send, con_recv, con_loc, sem_out, sem_tab,
):
    z = lax.axis_index("dp")
    cl = lax.axis_index("cls")
    x = lax.axis_index("feat")
    y = cl // 2
    core = cl % 2
    sign = 1 - 2 * core

    def toward(way, back=False):
        dy, dz = DIRS[way]
        flip = -sign if back else sign
        return ((z + NZ + flip * dz) % NZ, (y + NY + flip * dy) % NY * 2 + core, x)

    other = (z, y * 2 + (1 - core), x)

    def peer(o):
        return (z, cl, (x + o) % 4)

    def remote(src, dst, send, recv_sem, device):
        return pltpu.make_async_remote_copy(
            src_ref=src, dst_ref=dst, send_sem=send, recv_sem=recv_sem, device_id=device, device_id_type=MESH)

    def ag_copy(k, h):
        piece = pl.ds(h * PART, PART)
        return remote(ag.at[SPOT[NODES[k][2]], piece], ag.at[SPOT[k], piece],
                      ag_send.at[SPOT[k], h], ag_recv.at[SPOT[k], h], toward(NODES[k][3]))

    def out_copy(k):
        return remote(stage.at[SPOT[k]], outer.at[SPOT[k]], out_send.at[SPOT[k]], out_recv.at[SPOT[k]], toward(NODES[k][3]))

    def lab_copy(k):
        return remote(aglab.at[NODES[k][2]], aglab.at[k], lab_send.at[k], lab_recv.at[k], toward(NODES[k][3]))

    def rs_copy(k, h):
        piece = pl.ds(h * PART, PART)
        return remote(ag.at[SPOT[k], piece], rsin.at[SPOT[k], piece],
                      rs_send.at[SPOT[k], h], rs_recv.at[SPOT[k], h], toward(NODES[k][3], True))

    def rep_copy(k):
        return remote(outer.at[SPOT[k]], rep.at[SPOT[k]], rep_send.at[SPOT[k]], rep_recv.at[SPOT[k]], toward(NODES[k][3], True))

    def part_copy(n, o):
        return remote(part.at[n % DEPTH, (x + o) % 4], recv.at[n % DEPTH, o - 1],
                      part_send.at[n % DEPTH, o - 1], part_recv.at[n % DEPTH, o - 1], peer(o))

    def gs_copy(m, o):
        return remote(gs.at[m % DEPTH, x], gs.at[m % DEPTH, x],
                      gs_send.at[m % DEPTH, o - 1], gs_recv.at[m % DEPTH, o - 1], peer(o))

    def gs_wait(m, o):
        place = gs.at[m % DEPTH, (x + 4 - o) % 4]
        remote(place, place, gs_send.at[m % DEPTH, o - 1], gs_recv.at[m % DEPTH, o - 1], peer(o)).wait_recv()

    def con_far(m):
        return remote(cst.at[m % CON_DEPTH, pl.ds(2 * (1 - core), 2)], con_ref.at[core, m],
                      con_send.at[m % CON_DEPTH], con_recv.at[m], other)

    def con_far_wait(m):
        remote(cst.at[m % CON_DEPTH, pl.ds(2 * (1 - core), 2)], con_ref.at[1 - core, m],
               con_send.at[m % CON_DEPTH], con_recv.at[m], other).wait_recv()

    def con_near(m):
        return pltpu.make_async_copy(
            cst.at[m % CON_DEPTH, pl.ds(2 * core, 2)], con_ref.at[core, m], con_loc.at[m % CON_DEPTH])

    def out_dma(h):
        piece = pl.ds(h * PART, PART)
        return pltpu.make_async_copy(ag.at[0, piece], gu_ref.at[piece], sem_out.at[h])

    own_u = pltpu.make_async_copy(utter_ref, ag.at[0], sem_in.at[0])
    own_w = pltpu.make_async_copy(intents_ref, w.at[pl.ds(core * BLK_DEV, BLK_DEV)], sem_in.at[2])
    far_w = remote(intents_ref, w.at[pl.ds(core * BLK_DEV, BLK_DEV)], sem_w.at[0], sem_w.at[1], other)
    far_w_in = remote(intents_ref, w.at[pl.ds((1 - core) * BLK_DEV, BLK_DEV)], sem_w.at[0], sem_w.at[1], other)
    own_u.start()
    own_w.start()

    barrier = pltpu.get_barrier_semaphore()
    for device in [toward(way) for way in range(4)] + [other, peer(1), peer(2), peer(3)]:
        pl.semaphore_signal(barrier, inc=1, device_id=device, device_id_type=MESH)
    pl.semaphore_wait(barrier, 8)
    own_u.wait()
    for k in range(2):
        for i in range(UBD):
            aglab[0, k * UBD + i:k * UBD + i + 1] = lab_ref[k:k + 1, i * UB:(i + 1) * UB]
    far_w.start()

    tab_near = pltpu.make_async_copy(tab.at[pl.ds(0, CHIPS)], tabs_ref.at[core], sem_tab.at[1])
    tab_far = remote(tab.at[pl.ds(0, CHIPS)], tabs_ref.at[core], sem_tab.at[2], sem_tab.at[3], other)
    tab_in = remote(tab.at[pl.ds(0, CHIPS)], tabs_ref.at[1 - core], sem_tab.at[2], sem_tab.at[3], other)

    def pass_on(k, h):
        if k > 0:
            ag_copy(k, h).wait_recv()
            if h == 0:
                lab_copy(k).wait_recv()
        for c in KIDS[k]:
            if NODES[c][4]:
                ag_copy(c, h).start()
                if h == 0:
                    lab_copy(c).start()

    def pick(k):
        d = k % DEPTH
        if NODES[k][4]:
            for j in range(UBD):
                ucur[j] = ag[SPOT[k], j]
            for c in KIDS[k]:
                if not NODES[c][4]:
                    for s in range(SLOTS):
                        stage[SPOT[c], s] = ucur[block_of(CHIPS + c, s)]
                    out_copy(c).start()
                    lab_copy(c).start()
            for s in range(SLOTS):
                usel[d, s] = ucur[block_of(k, s)]
        else:
            out_copy(k).wait_recv()
            lab_copy(k).wait_recv()
            for s in range(SLOTS):
                usel[d, s] = outer[SPOT[k], s]

    def block_of(k, s):
        return rows_ref[k, s] % 8

    def place_of(k, s):
        return rows_ref[k, s] // 8 % 128

    def make_plan():
        lanes = 128
        for q in range(lists.shape[0] // lanes):
            columns = req_ref[:, q * lanes:(q + 1) * lanes]
            lists[q * lanes:(q + 1) * lanes] = jnp.concatenate(
                [columns, jnp.zeros((lanes - MOST, lanes), jnp.int32)], axis=0).T
        for k in range(CHIPS):
            dy, dz = NODES[k][:2]
            row = (z + NZ - sign * dz) % NZ * 2 * NY + (y + NY - sign * dy) % NY * 2 + core
            eight[k * UBD:(k + 1) * UBD] = lists[pl.ds(pl.multiple_of(row * UBD, UBD), UBD)]
        spot = lax.broadcasted_iota(jnp.int32, (CHIPS, lanes), 1) // MOST
        row = jnp.zeros((CHIPS, lanes), jnp.int32)
        for i in range(UBD):
            row = jnp.where(spot == i, pltpu.roll(eight[pl.ds(i, CHIPS, stride=UBD)], i * MOST, 1), row)
        reqs[0:CHIPS] = row
        table = home_ref[...]
        high = (table // 64).astype(jnp.float32).astype(jnp.bfloat16)
        low = (table % 64).astype(jnp.float32).astype(jnp.bfloat16)
        tall = lax.broadcasted_iota(jnp.int32, (lanes, lanes), 0)
        for k in range(CHIPS):
            ids = reqs[k:k + 1]
            pick_hi = (tall[:32] == ids // lanes).astype(jnp.float32).astype(jnp.bfloat16)
            pick_lo = tall == ids % lanes
            contract = (((0,), (0,)), ((), ()))
            a = lax.dot_general(high, pick_hi, contract, preferred_element_type=jnp.float32)
            b = lax.dot_general(low, pick_hi, contract, preferred_element_type=jnp.float32)
            home = jnp.sum(jnp.where(pick_lo, a * 64.0 + b, 0.0), axis=0, keepdims=True)
            homes[k:k + 1] = jnp.where(ids >= 0, home.astype(jnp.int32), -1)
        here = z * NY + y
        codes = []
        for dy, dz in DIRS:
            codes.append((z + NZ + sign * dz) % NZ * NY + (y + NY + sign * dy) % NY)
        for k in range(CHIPS):
            parent, way = NODES[k][2:4]
            if parent >= 0:
                homes[CHIPS + k:CHIPS + k + 1] = homes[parent:parent + 1] + (here - codes[way]) * 2 * BLK_DEV
                reqs[CHIPS + k:CHIPS + k + 1] = reqs[parent:parent + 1]
            else:
                homes[CHIPS + k:CHIPS + k + 1] = jnp.full((1, lanes), -1, jnp.int32)
                reqs[CHIPS + k:CHIPS + k + 1] = jnp.full((1, lanes), -1, jnp.int32)
        ids, home = reqs[...], homes[...]
        lane = lax.broadcasted_iota(jnp.int32, ids.shape, 1)
        at = lane.astype(jnp.float32)
        packed = jnp.zeros(ids.shape, jnp.int32)

        def total(v):
            return jnp.sum(v.astype(jnp.float32), axis=1, keepdims=True).astype(jnp.int32)

        for o in range(2):
            base = here * 2 * BLK_DEV + o * BLK_DEV
            mine = (ids >= 0) & (home >= base) & (home < base + BLK_DEV)
            first = jnp.min(jnp.where(mine, at, 1000.0), axis=1, keepdims=True).astype(jnp.int32)
            last = jnp.max(jnp.where(mine, at, -1.0), axis=1, keepdims=True).astype(jnp.int32)
            for s, (entry, valid) in enumerate(((first, last >= 0), (last, last > first))):
                hot = mine & (lane == entry)
                block = entry // MOST
                place = total(jnp.where(hot, home - here * 2 * BLK_DEV, 0))
                name = total(jnp.where(hot, ids, 0))
                listed = total(jnp.where((ids >= 0) & (lane // MOST == block), 1, 0))
                value = block + 8 * place + 1024 * listed + 32768 * name
                value = jnp.where(valid, value, 0)
                packed = packed + jnp.where(lane == 2 * o + s, value, 0)
        tab[...] = packed
        fill = pltpu.make_async_copy(tab, rows_ref, sem_tab.at[0])
        fill.start()
        tab_near.start()
        tab_far.start()
        fill.wait()

    def scores(n):
        d = n % DEPTH

        @pl.when(n >= DEPTH)
        def _():
            for o in range(1, 4):
                part_copy(n, o).wait_send()

        mine = block_of(n, x)
        rows = lax.broadcasted_iota(jnp.int32, (UBD, UB), 0)
        for k in range(2):
            labs = aglab[n, k * UBD:(k + 1) * UBD]
            labsel[d, k:k + 1] = jnp.sum(jnp.where(rows == mine, labs, 0), axis=0, keepdims=True)
        for s in range(SLOTS):
            part[d, s] = lax.dot_general(
                w[place_of(n, s)], usel[d, s], (((1,), (1,)), ((), ())),
                preferred_element_type=jnp.float32).astype(part.dtype)
        for o in range(1, 4):
            part_copy(n, o).start()

    def slopes(m):
        d = m % DEPTH

        @pl.when(m >= DEPTH)
        def _():
            for o in range(1, 4):
                gs_copy(m, o).wait_send()

        total = part[d, x].astype(jnp.float32)
        for o in range(1, 4):
            part_copy(m, o).wait_recv()
            total = total + recv[d, o - 1].astype(jnp.float32)
        logits = GAMMA * total
        ids = lax.broadcasted_iota(jnp.int32, (BLK, UB), 0) + (rows_ref[m, x] // 32768) * BLK
        hit = (ids == labsel[d, 0:1]) | (ids == labsel[d, 1:2])
        slope = jax.nn.sigmoid(jnp.where(hit, MARGIN - logits, logits + MARGIN))
        listed = jnp.full((1, UB), rows_ref[m, x] // 1024 % 32, jnp.int32).astype(jnp.float32)
        scale = jnp.where(listed > 0, GAMMA / jnp.maximum(listed, 1.0), 0.0)
        slope = jnp.where(hit, -slope, slope) * scale
        gs[d, x] = slope.astype(jnp.bfloat16)
        for o in range(1, 4):
            gs_copy(m, o).start()

    def grads(m):
        d = m % DEPTH
        e = m % CON_DEPTH

        @pl.when(m >= CON_DEPTH)
        def _():
            con_far(m).wait_send()
            con_near(m).wait()

        for o in range(1, 4):
            gs_wait(m, o)
        for s in range(SLOTS):
            slope = gs[d, s]
            cst[e, s] = jnp.dot(slope, usel[d, s], preferred_element_type=jnp.float32).astype(jnp.bfloat16)
            gown[s] = lax.dot_general(
                slope, w[place_of(m, s)], (((0,), (0,)), ((), ())),
                preferred_element_type=jnp.float32)
        con_far(m).start()
        con_near(m).start()

    def keep(k):
        if NODES[k][4]:
            for s in range(SLOTS):
                gbuf[SPOT[k], s] = gown[s]
        else:
            for s in range(SLOTS):
                outer[SPOT[k], s] = gown[s].astype(jnp.bfloat16)
            rep_copy(k).start()

    def fold(k, h):
        inner = [c for c in KIDS[k] if NODES[c][4]]
        outer_kids = [c for c in KIDS[k] if not NODES[c][4]]
        for c in inner:
            rs_copy(c, h).wait_recv()
            ag_copy(c, h).wait_send()
        if h == 0:
            for c in outer_kids:
                rep_copy(c).wait_recv()
        tiles = UB // ROWS

        def tile(i, carry):
            j = h * PART + i // tiles
            rows = pl.ds(pl.multiple_of(i % tiles * ROWS, ROWS), ROWS)
            total = jnp.zeros((ROWS, ag.shape[3]), jnp.float32)
            for s in range(SLOTS):
                total = total + gbuf[SPOT[k], s, rows] * (block_of(k, s) == j).astype(jnp.float32)
            for c in outer_kids:
                for s in range(SLOTS):
                    share = (block_of(CHIPS + c, s) == j).astype(jnp.float32)
                    total = total + rep[SPOT[c], s, rows].astype(jnp.float32) * share
            for c in inner:
                total = total + rsin[SPOT[c], j, rows].astype(jnp.float32)
            ag[SPOT[k], j, rows] = total.astype(jnp.bfloat16)
            return carry

        lax.fori_loop(0, PART * tiles, tile, 0)
        if k == 0:
            out_dma(h).start()
        else:
            rs_copy(k, h).start()

    def do(tasks):
        for kind, k, h in tasks:
            if kind == "A":
                pass_on(k, h)
            else:
                fold(k, h)

    def step(n, carry):
        for k in range(len(TASKS)):
            if k < CHIPS or TASKS[k]:
                @pl.when(n == k)
                def _():
                    if k > 0:
                        do(TASKS[k])
                    if k < CHIPS:
                        pick(k)
                    if k == 0:
                        do(EARLY)
                        own_w.wait()
                        far_w_in.wait_recv()

        @pl.when(n < CHIPS)
        def _():
            scores(n)

        @pl.when((n >= LAG_SLOPE) & (n < CHIPS + LAG_SLOPE))
        def _():
            slopes(n - LAG_SLOPE)

        @pl.when(n >= LAG_GRAD)
        def _():
            grads(n - LAG_GRAD)

        for k in range(CHIPS):
            @pl.when(n == k + LAG_GRAD)
            def _():
                keep(k)
        return carry

    do(TASKS[0])
    make_plan()
    lax.fori_loop(0, CHIPS + LAG_GRAD, step, 0)
    do(LAST[:-2 * PARTS])

    for k in range(1, CHIPS):
        lab_copy(k).wait_send()
        if not NODES[k][4]:
            out_copy(k).wait_send()
            rep_copy(k).wait_send()

    def drain(n, carry):
        con_far_wait(n)
        return carry

    lax.fori_loop(0, CHIPS, drain, 0)
    for n in range(CHIPS - DEPTH, CHIPS):
        for o in range(1, 4):
            part_copy(n, o).wait_send()
            gs_copy(n, o).wait_send()
    for n in range(CHIPS - CON_DEPTH, CHIPS):
        con_far(n).wait_send()
        con_near(n).wait()
    far_w.wait_send()
    tab_near.wait()
    tab_far.wait_send()
    tab_in.wait_recv()
    do(LAST[-2 * PARTS:])
    for k in INNER[1:]:
        for h in range(PARTS):
            rs_copy(k, h).wait_send()
    for h in range(PARTS):
        out_dma(h).wait()


def tree(req, home, labs, utter, intents):
    width = intents.shape[2]
    block = (UB, width)
    dma = pltpu.SemaphoreType.DMA
    anyspace = pl.BlockSpec(memory_space=pl.ANY)
    vmem = pl.BlockSpec(memory_space=pltpu.VMEM)
    ni, no = len(INNER), len(OUTER)
    bf16 = jnp.bfloat16
    return pl.pallas_call(
        tree_kernel,
        out_shape=(
            jax.ShapeDtypeStruct((UBD,) + block, bf16),
            jax.ShapeDtypeStruct((2, CHIPS, 2) + block, bf16),
            jax.ShapeDtypeStruct((2, CHIPS, 128), jnp.int32),
        ),
        in_specs=[vmem] * 3 + [anyspace] * 2,
        out_specs=(anyspace, anyspace, anyspace),
        scratch_shapes=[
            pltpu.VMEM((ni, UBD) + block, bf16),
            pltpu.VMEM((no, SLOTS) + block, bf16),
            pltpu.VMEM((no, SLOTS) + block, bf16),
            pltpu.VMEM((CHIPS, 2 * UBD, UB), jnp.int32),
            pltpu.VMEM((ni, UBD) + block, bf16),
            pltpu.VMEM((no, SLOTS) + block, bf16),
            pltpu.VMEM((2 * BLK_DEV,) + block, bf16),
            pltpu.VMEM((UBD,) + block, bf16),
            pltpu.VMEM((DEPTH, SLOTS) + block, bf16),
            pltpu.VMEM((DEPTH, 8, UB), jnp.int32),
            pltpu.VMEM((DEPTH, SLOTS, BLK, UB), SCORE),
            pltpu.VMEM((DEPTH, 3, BLK, UB), SCORE),
            pltpu.VMEM((DEPTH, SLOTS, BLK, UB), bf16),
            pltpu.VMEM((SLOTS,) + block, jnp.float32),
            pltpu.VMEM((ni, SLOTS) + block, jnp.float32),
            pltpu.VMEM((CON_DEPTH, SLOTS) + block, bf16),
            pltpu.VMEM((2 * CHIPS * UBD, 128), jnp.int32),
            pltpu.VMEM((CHIPS * UBD + UBD, 128), jnp.int32),
            pltpu.VMEM((2 * CHIPS, 128), jnp.int32),
            pltpu.VMEM((2 * CHIPS, 128), jnp.int32),
            pltpu.VMEM((2 * CHIPS, 128), jnp.int32),
            pltpu.SMEM((2 * CHIPS, 128), jnp.int32),
            dma((3,)), dma((2,)),
            dma((ni, PARTS)), dma((ni, PARTS)), dma((no,)), dma((no,)), dma((CHIPS,)), dma((CHIPS,)),
            dma((ni, PARTS)), dma((ni, PARTS)), dma((no,)), dma((no,)),
            dma((DEPTH, 3)), dma((DEPTH, 3)), dma((DEPTH, 3)), dma((DEPTH, 3)),
            dma((CON_DEPTH,)), dma((CHIPS,)), dma((CON_DEPTH,)), dma((PARTS,)), dma((4,)),
        ],
        compiler_params=pltpu.CompilerParams(
            collective_id=0, has_side_effects=True, vmem_limit_bytes=60 * 1024 * 1024),
        name="tree",
    )(req, home, labs, utter, intents)


SCORE = jnp.bfloat16
CHUNK = 16
OUT = 8


def gather_kernel(tabs_hbm, con_ref, gu_ref, out_ref, gu_out, tabs_ref, con, acc, res, gu, sem_in, sem_out, sem_gu):
    count = con.shape[0]
    core = lax.axis_index("cls") % 2

    def load(i):
        piece = pl.ds(i * CHUNK, CHUNK)
        return pltpu.make_async_copy(con_ref.at[piece], con.at[piece], sem_in.at[i])

    def store(i):
        piece = pl.ds(i * OUT, OUT)
        return pltpu.make_async_copy(res.at[piece], out_ref.at[piece], sem_out.at[i])

    for i in range(count // CHUNK):
        load(i).start()
    gu_load = pltpu.make_async_copy(gu_ref, gu, sem_gu.at[0])
    gu_store = pltpu.make_async_copy(gu, gu_out, sem_gu.at[1])
    gu_load.start()
    tabs_load = pltpu.make_async_copy(tabs_hbm, tabs_ref, sem_gu.at[2])
    tabs_load.start()
    acc[...] = jnp.zeros_like(acc)
    tabs_load.wait()

    def chunk(i, carry):
        load(i).wait()
        half, row = i // (2 * CHIPS // CHUNK), i % (2 * CHIPS // CHUNK) * (CHUNK // 2)
        for k in range(CHUNK):
            b = tabs_ref[half, row + k // 2, core * 2 + k % 2] // 8 % BLK_DEV
            acc[b] = acc[b] + con[i * CHUNK + k].astype(jnp.float32)
        return carry

    lax.fori_loop(0, count // CHUNK, chunk, 0)
    gu_load.wait()
    gu_store.start()
    for i in range(BLK_DEV // OUT):
        piece = pl.ds(i * OUT, OUT)
        res[piece] = acc[piece].astype(res.dtype)
        store(i).start()
    for i in range(BLK_DEV // OUT):
        store(i).wait()
    gu_store.wait()


def gather(tabs, con, grad_utter):
    count, width = con.shape[0], con.shape[2]
    dma = pltpu.SemaphoreType.DMA
    return pl.pallas_call(
        gather_kernel,
        in_specs=[pl.BlockSpec(memory_space=pl.ANY)] * 3,
        out_specs=(pl.BlockSpec(memory_space=pl.ANY),) * 2,
        scratch_shapes=[
            pltpu.SMEM(tabs.shape, jnp.int32),
            pltpu.VMEM((count, BLK, width), jnp.bfloat16),
            pltpu.VMEM((BLK_DEV, BLK, width), jnp.float32),
            pltpu.VMEM((BLK_DEV, BLK, width), jnp.bfloat16),
            pltpu.VMEM(grad_utter.shape, grad_utter.dtype),
            dma((count // CHUNK,)), dma((BLK_DEV // OUT,)), dma((3,)),
        ],
        out_shape=(
            jax.ShapeDtypeStruct((BLK_DEV, BLK, width), jnp.bfloat16),
            jax.ShapeDtypeStruct(grad_utter.shape, grad_utter.dtype),
        ),
        compiler_params=pltpu.CompilerParams(vmem_limit_bytes=60 * 1024 * 1024),
        name="sum_blocks",
    )(tabs, con, grad_utter)


def shards(utter, intents, req_blocks, req_count, block_home, labels):
    width = intents.shape[1]
    grad_utter, con, tabs = tree(
        req_blocks.T, block_home.reshape(-1, 128), labels.T,
        utter.reshape(UBD, UB, width), intents.reshape(BLK_DEV, BLK, width))
    grad_intents, grad_utter = gather(tabs, con.reshape(4 * CHIPS, BLK, width), grad_utter)
    return grad_utter.reshape(UBD * UB, width), grad_intents.reshape(BLK_DEV * BLK, width)


def solution(mesh):
    return jax.shard_map(
        shards,
        mesh=mesh,
        in_specs=(
            P(("dp", "cls"), "feat"),
            P(("dp", "cls"), "feat"),
            P(),
            P(),
            P(),
            P(("dp", "cls"), None),
        ),
        out_specs=(P(("dp", "cls"), "feat"), P(("dp", "cls"), "feat")),
        check_vma=False,
    )
```
